256 devices in a mesh: grp: 8 (over z_lo, y), seq: 4 (over z_hi), smp: 8 (over x, core).
Axes of the slice: x: 4, y: 4, z: 8 (z_hi: 4, z_lo: 2; z = z_hi * 2 + z_lo), core: 2. Of those that a mesh axis runs over, the one named last changes fastest.
Arguments:
- prompt_x: bfloat16 [16384, 5120], P(('grp', 'seq')), parts along dimension 0, may hold values from -6 to 6
- sampled_x: bfloat16 [128, 4, 5120], P('grp'), parts along dimension 0, may hold values from -6 to 6
- w_query: bfloat16 [5120, 8192], P('seq', 'smp'), may hold values from -0.078125 to 0.078125
- w_key: bfloat16 [5120, 1024], P('seq', 'smp'), may hold values from -0.078125 to 0.078125
- w_value: bfloat16 [5120, 1024], P('seq', 'smp'), may hold values from -0.078125 to 0.078125
- q_gain: float32 [128], replicated, may hold values from 0.25 to 1.75
- k_gain: float32 [128], replicated, may hold values from 0.25 to 1.75
Outputs:
- prefill_out: bfloat16 [16384, 8192], P(('grp', 'seq'), 'smp'), parts along dimension 0
- decode_out: bfloat16 [128, 4, 8192], P(('grp', 'smp')), parts along dimension 0
The draws below stay inside these ranges and needn't reach their ends.
There are 8 independent parts, one for each index of `grp`. The reference program is written for one: setup_inputs(seed, part) draws one part's arguments, and reference() takes and returns one part's arrays. A program takes and returns all parts, laid end to end along the dimension named above; an argument that names none is the same for every part. Nothing has to cross between parts.
All inputs are finite; a program needn't handle non-finite values.
Results may differ from the reference program's by a relative error of at most 0.023.
Values may be sent and summed in bfloat16 or wider, within the bound.
A program may use at most 128 MiB of HBM per device.

```python
import jax
import jax.numpy as jnp
from jax import lax

D = 5120
HQ = 64
HK = 8
HD = 128
STEPS = 4
PROMPT = 2048
SAMPLES = 16


def steps_of(rng, dims, split, low, top_value):
    def one(dim, shards_of):
        steps = jax.random.uniform(jax.random.fold_in(jax.random.fold_in(rng, 6), dim), (shards_of,), jnp.float32, low / len(split), top_value / len(split))
        return jnp.repeat(jnp.exp(steps), dims[dim] // shards_of).reshape((-1,) + (1,) * (len(dims) - dim - 1))

    factor_of = one(*split[0])
    for cut in split[1:]:
        factor_of = factor_of * one(*cut)
    return factor_of


def scatter_about(rng, shape, deviation, bound, split=(), held_as=jnp.bfloat16):
    array = jax.random.normal(rng, shape, jnp.float32) * deviation
    if len(split) > 0:
        array = steps_of(rng, shape, split, -0.22, 0.18) * array
    return jnp.clip(array, min=-bound, max=bound).astype(held_as)


def setup_inputs(seed: int = 0, part: int = 0) -> dict:
    seeds = jax.random.split(jax.random.key(seed), 8)
    part_splits = jax.random.split(jax.random.fold_in(seeds[7], part), 8)
    prompt_x = scatter_about(part_splits[0], (PROMPT, D), 1.0, 6.0, ((0, 4),))
    sampled_x = scatter_about(part_splits[1], (SAMPLES, STEPS, D), 1.0, 6.0)
    w_query = scatter_about(seeds[2], (D, HQ * HD), D ** -0.5, 0.078125, ((0, 4), (1, 8)))
    w_key = scatter_about(seeds[3], (D, HK * HD), D ** -0.5, 0.078125, ((0, 4), (1, 8)))
    w_value = scatter_about(seeds[4], (D, HK * HD), D ** -0.5, 0.078125, ((0, 4), (1, 8)))
    q_gain = jnp.clip(1.0 + 0.15 * jax.random.normal(seeds[5], (HD,), jnp.float32), 0.25, 1.75)
    k_gain = jnp.clip(1.0 + 0.15 * jax.random.normal(seeds[6], (HD,), jnp.float32), 0.25, 1.75)
    return {"prompt_x": prompt_x, "sampled_x": sampled_x, "w_query": w_query, "w_key": w_key, "w_value": w_value, "q_gain": q_gain, "k_gain": k_gain}


neg_fill = -1e+30

def rope_parts(positions):
    half = HD // 2
    freq = 1000000.0 ** (-(jnp.arange(half, dtype=jnp.float32) * 2.0 / HD))
    angle = positions.astype(jnp.float32)[:, None] * freq[None, :]
    return (jnp.cos(angle), jnp.sin(angle))

def norm_rotate(values, gain, positions):
    scaled = values * lax.rsqrt(lax.optimization_barrier(jnp.mean(values * values, -1, keepdims=True)) + 1e-06) * gain
    cosine, sine = rope_parts(positions)
    cosine = cosine[:, None, :]
    sine = sine[:, None, :]
    first = scaled[..., :HD // 2]
    second = scaled[..., HD // 2:]
    return jnp.concatenate([first * cosine - second * sine, second * cosine + first * sine], -1)

def project(inputs, w_query, w_key, w_value, q_gain, k_gain, positions):
    count = inputs.shape[0]
    query = jnp.dot(inputs, w_query, preferred_element_type=jnp.float32).reshape(count, -1, HD)
    key = jnp.dot(inputs, w_key, preferred_element_type=jnp.float32).reshape(count, -1, HD)
    value = jnp.dot(inputs, w_value, preferred_element_type=jnp.float32).reshape(count, -1, HD)
    return (norm_rotate(query, q_gain, positions).astype(jnp.bfloat16), norm_rotate(key, k_gain, positions).astype(jnp.bfloat16), value.astype(jnp.bfloat16))

def reference(prompt_x, sampled_x, w_query, w_key, w_value, q_gain, k_gain):
    length = prompt_x.shape[0]
    samples, steps, width = sampled_x.shape
    group = HQ // HK
    scale = HD ** (-0.5)
    query, key, value = project(prompt_x, w_query, w_key, w_value, q_gain, k_gain, jnp.arange(length, dtype=jnp.int32))
    block = min(512, length)
    query_four = query.reshape(length, HK, group, HD)
    keys_wide = key.astype(jnp.float32)
    values_wide = value.astype(jnp.float32)

    def one_block(index):
        start = index * block
        rows_q = lax.dynamic_slice_in_dim(query_four, start, block, 0).astype(jnp.float32)
        scores = jnp.einsum('bkgd,lkd->kgbl', rows_q, keys_wide) * scale
        allowed = jnp.arange(length, dtype=jnp.int32)[None, :] <= (start + jnp.arange(block, dtype=jnp.int32))[:, None]
        scores = jnp.where(allowed, scores, neg_fill)
        top = scores.max(-1, keepdims=True)
        prob = jnp.where(allowed, jnp.exp(scores - top), 0.0)
        total = prob.sum(-1)
        weights = lax.optimization_barrier(prob.astype(jnp.bfloat16)).astype(jnp.float32)
        out = jnp.einsum('kgbl,lkd->bkgd', weights, values_wide) / jnp.transpose(total, (2, 0, 1))[..., None]
        return out.astype(jnp.bfloat16)
    prefill = lax.map(one_block, jnp.arange(length // block, dtype=jnp.int32)).reshape(length, HQ * HD)
    flat = sampled_x.reshape(samples * steps, width)
    positions = jnp.tile(length + jnp.arange(steps, dtype=jnp.int32), samples)
    dec_q, dec_k, dec_v = project(flat, w_query, w_key, w_value, q_gain, k_gain, positions)
    dec_q = dec_q.reshape(samples, steps, HK, group, HD).astype(jnp.float32)
    dec_k = dec_k.reshape(samples, steps, HK, HD).astype(jnp.float32)
    dec_v = dec_v.reshape(samples, steps, HK, HD).astype(jnp.float32)
    prompt_scores = jnp.einsum('stkgd,lkd->stkgl', dec_q, keys_wide) * scale
    own_scores = jnp.einsum('stkgd,sukd->stkgu', dec_q, dec_k) * scale
    allowed = jnp.arange(steps)[None, :] <= jnp.arange(steps)[:, None]
    mask_six = allowed[None, :, None, None, :]
    own_scores = jnp.where(mask_six, own_scores, neg_fill)
    top = jnp.maximum(prompt_scores.max(-1), own_scores.max(-1))[..., None]
    prompt_prob = jnp.exp(prompt_scores - top)
    own_prob = jnp.where(mask_six, jnp.exp(own_scores - top), 0.0)
    total = prompt_prob.sum(-1) + own_prob.sum(-1)
    prompt_w = lax.optimization_barrier(prompt_prob.astype(jnp.bfloat16)).astype(jnp.float32)
    own_w = lax.optimization_barrier(own_prob.astype(jnp.bfloat16)).astype(jnp.float32)
    acc = jnp.einsum('stkgl,lkd->stkgd', prompt_w, values_wide) + jnp.einsum('stkgu,sukd->stkgd', own_w, dec_v)
    decode = (acc / total[..., None]).astype(jnp.bfloat16).reshape(samples, steps, HQ * HD)
    return (prefill, decode)
```

```python
import functools
import math

import jax
import jax.numpy as jnp
import numpy as np
from jax import lax
from jax.experimental import pallas as pl
from jax.experimental.pallas import tpu as pltpu
from jax.sharding import PartitionSpec as P

HD = 128
MESH = pl.DeviceIdType.MESH
N_Y = 4
N_SEQ = 4
N_SMP = 8
WINDOW = 4
LAG = 4
I1, J1, I2, J2, YA, YB, YC = 0, 1, 2, 3, 4, 6, 8


def dot_t(a, b):
    return lax.dot_general(a, b, (((1,), (1,)), ((), ())), preferred_element_type=jnp.float32)


def kernel(
    px_ref, sx_ref, wq_ref, wk_ref, wv_ref, qg_ref, kg_ref, freq_ref,
    out_ref, dec_ref,
    xb, w, proj, tabs, kvx, vaug, kvd, qbuf, acc, obuf, dsend, drecv,
    load_sem, send_sem, recv_sem, kv_send, kv_recv, o_sem, d_send, d_recv,
):
    rows = px_ref.shape[0]
    drows = sx_ref.shape[0]
    depth = wq_ref.shape[0]
    heads = wq_ref.shape[1] // HD
    slots = heads + 2
    count = rows + drows
    half = depth // 2
    quarter = depth // 4
    grp = lax.axis_index("grp")
    seq = lax.axis_index("seq")
    smp = lax.axis_index("smp")
    lo = grp // N_Y
    y = lax.rem(grp, N_Y)
    par = lax.rem(y, 2)
    up = lax.rem(seq + 1, N_SEQ)
    down = lax.rem(seq + N_SEQ - 1, N_SEQ)
    far = lax.rem(seq + 2, N_SEQ)
    near = lax.rem(seq + 2 * lo + N_SEQ - 1, N_SEQ)
    other = lax.rem(seq + N_SEQ + 1 - 2 * lo, N_SEQ)
    lo_grp = (1 - lo) * N_Y + y
    inter = (lo_grp, near, smp)
    intra = (lo_grp, seq, smp)
    y_up = lax.rem(y + 1, N_Y)
    y_down = lax.rem(y + N_Y - 1, N_Y)
    y_dev = ((lo * N_Y + y_up, seq, smp), (lo * N_Y + y_down, seq, smp))
    y_mine = (lo * N_Y + lax.rem(y + 1 + 2 * lo, N_Y), seq, smp)
    y_rest = (lo * N_Y + lax.rem(y + 3 - 2 * lo, N_Y), seq, smp)
    seq_dev = ((grp, up, smp), (grp, down, smp))

    loads = []
    loads.append(pltpu.make_async_copy(wk_ref, w.at[0, pl.ds(seq * depth, depth)], load_sem.at[0]))
    loads.append(pltpu.make_async_copy(wv_ref, w.at[1, pl.ds(seq * depth, depth)], load_sem.at[1]))
    for h in range(heads):
        loads.append(
            pltpu.make_async_copy(
                wq_ref.at[:, pl.ds(h * HD, HD)], w.at[2 + h, pl.ds(seq * depth, depth)], load_sem.at[2 + h]
            )
        )
    loads.append(pltpu.make_async_copy(px_ref, xb.at[pl.ds(0, rows)], load_sem.at[slots]))
    loads.append(pltpu.make_async_copy(sx_ref, xb.at[pl.ds(rows, drows)], load_sem.at[slots + 1]))
    for load in loads:
        load.start()

    barrier = pltpu.get_barrier_semaphore()
    for dev in (inter, intra) + y_dev + seq_dev:
        pl.semaphore_signal(barrier, inc=1, device_id=dev, device_id_type=MESH)
    for d in range(1, N_SMP):
        pl.semaphore_signal(
            barrier, inc=1, device_id=(grp, seq, lax.rem(smp + d, N_SMP)), device_id_type=MESH
        )
    pl.semaphore_wait(barrier, 6 + N_SMP - 1)

    def piece(slot, block, start, size):
        return w.at[slot, pl.ds(pl.multiple_of(block * depth + start, 16), size)]

    def message(slot, kind, block, start, size, dev):
        ref = piece(slot, block, start, size)
        return pltpu.make_async_remote_copy(
            src_ref=ref, dst_ref=ref, send_sem=send_sem.at[slot, kind], recv_sem=recv_sem.at[slot, kind],
            device_id=dev, device_id_type=MESH,
        )

    mine = par * half
    theirs = (1 - par) * half

    def send_i1(slot):
        message(slot, I1, seq, mine, half, inter).start()

    def send_y(slot, kind, block):
        for q in range(2):
            message(slot, kind + q, block, mine + q * quarter, quarter, y_dev[q]).start()

    def arrived(slot, kind, block, start, size):
        message(slot, kind, block, start, size, inter).wait_recv()

    for slot in range(WINDOW):
        loads[slot].wait()
        send_i1(slot)
    for slot in range(WINDOW, slots):
        loads[slot].wait()

    row = lax.broadcasted_iota(jnp.int32, (count, HD), 0)
    lane = lax.broadcasted_iota(jnp.int32, (count, HD), 1)
    position = jnp.where(row < rows, seq * rows + row, N_SEQ * rows + lax.rem(row - rows, 4))
    angle = position.astype(jnp.float32) * freq_ref[...]
    cosine = jnp.cos(angle)
    sine = jnp.sin(angle)
    sine = jnp.where(lane < HD // 2, -sine, sine)
    fold = HD ** (-0.5) * math.log2(math.e)
    for n, (gain_ref, factor) in enumerate(((kg_ref, 1.0), (qg_ref, fold))):
        gain = gain_ref[...] * factor
        tabs[n, 0] = cosine * gain
        tabs[n, 1] = sine * pltpu.roll(gain, HD // 2, 1)
    vaug[:, :, HD:] = jnp.ones((N_SEQ, rows, HD), jnp.bfloat16)
    kvd[1, :, HD:] = jnp.ones((drows, HD), jnp.bfloat16)
    loads[slots].wait()
    loads[slots + 1].wait()

    def rotated(n):
        u = proj[...]
        r = lax.rsqrt(jnp.mean(u * u, -1, keepdims=True) + 1e-6)
        return (r * (u * tabs[n, 0] + pltpu.roll(u, HD // 2, 1) * tabs[n, 1])).astype(jnp.bfloat16)

    def kv_message(n, src, dev):
        return pltpu.make_async_remote_copy(
            src_ref=src, dst_ref=src, send_sem=kv_send.at[n], recv_sem=kv_recv.at[n], device_id=dev, device_id_type=MESH
        )

    def kv_up():
        return kv_message(0, kvx.at[seq], seq_dev[0])

    def kv_down():
        return kv_message(1, kvx.at[seq], seq_dev[1])

    def kv_far_up():
        return kv_message(2, kvx.at[down, 0], seq_dev[0])

    def kv_far_down():
        return kv_message(3, kvx.at[up, 1], seq_dev[1])

    def out_copy(h):
        return pltpu.make_async_copy(
            obuf.at[h], out_ref.at[:, pl.ds(pl.multiple_of(h * HD, HD), HD)], o_sem.at[h]
        )

    def attend(h):
        q = qbuf[h, pl.ds(0, rows)]
        scores = dot_t(q, kvx[seq, 0])
        allowed = lax.broadcasted_iota(jnp.int32, (rows, rows), 1) <= lax.broadcasted_iota(jnp.int32, (rows, rows), 0)
        e = jnp.where(allowed, jnp.exp2(scores), 0.0).astype(jnp.bfloat16)
        acc[...] = jnp.dot(e, vaug[seq], preferred_element_type=jnp.float32)

        def block(j, _):
            p = jnp.exp2(dot_t(q, kvx[j, 0])).astype(jnp.bfloat16)
            acc[...] += jnp.dot(p, vaug[j], preferred_element_type=jnp.float32)
            return 0

        lax.fori_loop(0, seq, block, 0)
        obuf[h] = (acc[:, :HD] / acc[:, HD:]).astype(jnp.bfloat16)
        out_copy(h).start()

        qd = qbuf[h, pl.ds(rows, drows)]
        a = lax.broadcasted_iota(jnp.int32, (drows, drows), 0)
        b = lax.broadcasted_iota(jnp.int32, (drows, drows), 1)
        own = jnp.where((b <= a) & (a // 4 == b // 4), jnp.exp2(dot_t(qd, kvd[0, :, :HD])), 0.0)
        total = jnp.dot(own.astype(jnp.bfloat16), kvd[1], preferred_element_type=jnp.float32)
        for j in range(N_SEQ):
            p = jnp.exp2(dot_t(qd, kvx[j, 0])).astype(jnp.bfloat16)
            total += jnp.dot(p, vaug[j], preferred_element_type=jnp.float32)
        res = total[:, :HD] / total[:, HD:]
        dsend[:, :, pl.ds(pl.multiple_of(h * HD, HD), HD)] = res.reshape(N_SMP, drows // N_SMP, HD)

    first_att = LAG + 4

    def done_by(i):
        return jnp.clip(jnp.where(i > first_att, i - LAG - 1, jnp.where(i == first_att, 2, 0)), 0, heads)

    def step(i, _):
        @pl.when(i < slots)
        def _():
            arrived(i, I1, near, mine, half)
            message(i, J1, near, mine, half, intra).start()
            send_y(i, YA, near)

        @pl.when(i + WINDOW < slots)
        def _():
            send_i1(i + WINDOW)

        @pl.when((i >= 1) & (i - 1 < slots))
        def _():
            t = i - 1
            arrived(t, J1, other, mine, half)
            message(t, I2, other, mine + (1 - lo) * quarter, quarter, inter).start()
            send_y(t, YB, other)

        @pl.when((i >= 2) & (i - 2 < slots))
        def _():
            t = i - 2
            arrived(t, I2, far, mine + lo * quarter, quarter)
            message(t, J2, far, mine + lo * quarter, quarter, intra).start()
            message(t, YC + lo, far, mine + lo * quarter, quarter, y_mine).start()

        @pl.when((i >= 3) & (i - 3 < slots))
        def _():
            t = i - 3
            arrived(t, J2, far, mine + (1 - lo) * quarter, quarter)
            message(t, YC + 1 - lo, far, mine + (1 - lo) * quarter, quarter, y_rest).start()

        @pl.when(i == LAG + 2)
        def _():
            kv_up().wait_recv()
            kv_far_up().start()
            kv_down().wait_recv()
            kv_far_down().start()

        @pl.when(i >= LAG)
        def _():
            t = i - LAG
            for q in range(2):
                arrived(t, YA + q, near, theirs + q * quarter, quarter)
                arrived(t, YB + q, other, theirs + q * quarter, quarter)
                arrived(t, YC + q, far, theirs + q * quarter, quarter)
            proj[...] = jnp.dot(xb[...], w[t], preferred_element_type=jnp.float32)

            @pl.when(t == 0)
            def _():
                k = rotated(0)
                kvx[seq, 0] = k[:rows]
                kvd[0, :, :HD] = k[rows:]

            @pl.when(t == 1)
            def _():
                v = proj[...].astype(jnp.bfloat16)
                kvx[seq, 1] = v[:rows]
                kvd[1, :, :HD] = v[rows:]
                kv_up().start()
                kv_down().start()

            @pl.when(t >= 2)
            def _():
                qbuf[t - 2] = rotated(1)

        @pl.when(i == first_att)
        def _():
            kv_message(2, kvx.at[far, 0], seq_dev[0]).wait_recv()
            kv_message(3, kvx.at[far, 1], seq_dev[1]).wait_recv()
            vaug[:, :, :HD] = kvx[:, 1]

        def one(h, _):
            attend(h)
            return 0

        lax.fori_loop(done_by(i - 1), done_by(i), one, 0)
        return 0

    lax.fori_loop(0, slots + LAG, step, 0)

    def d_message(d, target):
        return pltpu.make_async_remote_copy(
            src_ref=dsend.at[target], dst_ref=drecv.at[smp], send_sem=d_send.at[d], recv_sem=d_recv.at[d],
            device_id=(grp, seq, target), device_id_type=MESH,
        )

    for d in range(1, N_SMP):
        d_message(d, lax.rem(smp + d, N_SMP)).start()
    drecv[smp] = dsend[smp]

    def sent(slot, _):
        for kind, size in ((I1, half), (J1, half), (I2, quarter), (J2, quarter)):
            message(slot, kind, seq, 0, size, inter).wait_send()
        for kind in range(YA, YC + 2):
            message(slot, kind, seq, 0, quarter, inter).wait_send()
        return 0

    lax.fori_loop(0, slots, sent, 0)
    kv_up().wait_send()
    kv_down().wait_send()
    kv_far_up().wait_send()
    kv_far_down().wait_send()
    for h in range(heads):
        out_copy(h).wait()
    for d in range(1, N_SMP):
        d_message(d, lax.rem(smp + d, N_SMP)).wait_send()
    for d in range(1, N_SMP):
        d_message(d, lax.rem(smp + N_SMP - d, N_SMP)).wait_recv()
    cols = heads * HD
    for j in range(N_SMP):
        dec_ref[:, j * cols : (j + 1) * cols] = drecv[j]


def local(prompt_x, sampled_x, w_query, w_key, w_value, q_gain, k_gain):
    rows, width = prompt_x.shape
    samples, steps, _ = sampled_x.shape
    drows = samples * steps
    depth, q_cols = w_query.shape
    heads = q_cols // HD
    slots = heads + 2
    count = rows + drows
    mine = drows // N_SMP
    half = np.arange(HD // 2, dtype=np.float64)
    freq = 1e6 ** (-2.0 * half / HD)
    freq = jnp.asarray(np.concatenate([freq, freq]).reshape(1, HD).astype(np.float32))
    any_spec = pl.BlockSpec(memory_space=pl.ANY)
    vmem = pl.BlockSpec(memory_space=pltpu.VMEM)
    prefill, dec = pl.pallas_call(
        kernel,
        out_shape=(
            jax.ShapeDtypeStruct((rows, q_cols), jnp.bfloat16),
            jax.ShapeDtypeStruct((mine, N_SMP * q_cols), jnp.float32),
        ),
        in_specs=[any_spec] * 5 + [vmem] * 3,
        out_specs=(any_spec, vmem),
        scratch_shapes=[
            pltpu.VMEM((count, width), jnp.bfloat16),
            pltpu.VMEM((slots, width, HD), jnp.bfloat16),
            pltpu.VMEM((count, HD), jnp.float32),
            pltpu.VMEM((2, 2, count, HD), jnp.float32),
            pltpu.VMEM((N_SEQ, 2, rows, HD), jnp.bfloat16),
            pltpu.VMEM((N_SEQ, rows, 2 * HD), jnp.bfloat16),
            pltpu.VMEM((2, drows, 2 * HD), jnp.bfloat16),
            pltpu.VMEM((heads, count, HD), jnp.bfloat16),
            pltpu.VMEM((rows, 2 * HD), jnp.float32),
            pltpu.VMEM((heads, rows, HD), jnp.bfloat16),
            pltpu.VMEM((N_SMP, mine, q_cols), jnp.float32),
            pltpu.VMEM((N_SMP, mine, q_cols), jnp.float32),
            pltpu.SemaphoreType.DMA((slots + 2,)),
            pltpu.SemaphoreType.DMA((slots, 10)),
            pltpu.SemaphoreType.DMA((slots, 10)),
            pltpu.SemaphoreType.DMA((4,)),
            pltpu.SemaphoreType.DMA((4,)),
            pltpu.SemaphoreType.DMA((heads,)),
            pltpu.SemaphoreType.DMA((N_SMP,)),
            pltpu.SemaphoreType.DMA((N_SMP,)),
        ],
        compiler_params=pltpu.CompilerParams(
            collective_id=0, has_side_effects=True, vmem_limit_bytes=48 * 2**20
        ),
    )(
        prompt_x, sampled_x.reshape(drows, width), w_query, w_key, w_value,
        q_gain.reshape(1, HD), k_gain.reshape(1, HD), freq,
    )
    return prefill, dec.astype(jnp.bfloat16).reshape(samples // N_SMP, steps, N_SMP * q_cols)


def solution(mesh):
    in_specs = (
        P(("grp", "seq"), None),
        P("grp", None, None),
        P("seq", "smp"),
        P("seq", "smp"),
        P("seq", "smp"),
        P(),
        P(),
    )
    out_specs = (P(("grp", "seq"), "smp"), P(("grp", "smp"), None, None))
    return jax.shard_map(local, mesh=mesh, in_specs=in_specs, out_specs=out_specs, check_vma=False)
```

```python
import math

import jax
import jax.numpy as jnp
from jax import lax
from jax.experimental import pallas as pl
from jax.experimental.pallas import tpu as pltpu
from jax.sharding import PartitionSpec as P

HD = 128
PAIR = 2 * HD
MESH = pl.DeviceIdType.MESH
N_Y = 4
N_SEQ = 4
N_SMP = 8
N_X = N_SMP // 2
SUBS = 5
X_CUTS = 4
WINDOW = 2
AT_J1 = 1
AT_I2 = 2
AT_J2 = 3
LAG = 5
KV_ON = 13
KV_END = 15
X_START = (3, 5, 7, 9)
X_STEPS = (11, 15, 19, 23, 16, 20, 24, 27, 28, 30)
PARTNER_AT = (15, 15, 16, 16, 16, 17, 17, 18, 18, 19)
ATTEND_AT = (15, 16, 19, 19, 19, 19, 19, 19)
I1, J1, I2, J2, Y = 0, 1, 2, 3, 4


def reached(i, steps):
    return sum((i >= step).astype(jnp.int32) for step in steps)


def chunk_at(i):
    third, rest = i // 3, lax.rem(i, 3)
    return jnp.where(i < SUBS + SUBS // 2, jnp.where(rest == 2, SUBS + third, 2 * third + rest), i)


def dot(a, b):
    return jnp.dot(a, b, preferred_element_type=jnp.float32)


def dot_t(a, b):
    return lax.dot_general(a, b, (((1,), (1,)), ((), ())), preferred_element_type=jnp.float32)


def kernel(
    px_ref, sx_ref, wq_ref, wk_ref, wv_ref, qg_ref, kg_ref,
    out_ref, dout_ref,
    xb, xp, sxb, w, proj, projp, qsend, tabs, gains, kvx, vaug, kvd, qbuf, obuf, dsend, dec_ref,
    load_sem, x_sem, o_sem, send_sem, recv_sem, kv_send, kv_recv, d_send, d_recv, xs_send, xs_recv, q_send, q_recv,
):
    rows = px_ref.shape[0]
    drows = sx_ref.shape[0] * sx_ref.shape[1]
    heads = wq_ref.shape[1] // HD
    shared = heads // 2
    depth = wq_ref.shape[0] // SUBS
    width = N_SEQ * depth
    chunks = SUBS * (1 + shared // 2)
    count = rows + drows
    half = depth // 2
    quarter = depth // 4
    grp = lax.axis_index("grp")
    seq = lax.axis_index("seq")
    smp = lax.axis_index("smp")
    lo = grp // N_Y
    y = lax.rem(grp, N_Y)
    par = lax.rem(y, 2)
    up = lax.rem(seq + 1, N_SEQ)
    down = lax.rem(seq + N_SEQ - 1, N_SEQ)
    far = lax.rem(seq + 2, N_SEQ)
    mirror = N_SEQ - 1 - seq
    near = lax.rem(seq + 2 * lo + N_SEQ - 1, N_SEQ)
    other = lax.rem(seq + N_SEQ + 1 - 2 * lo, N_SEQ)
    lo_grp = (1 - lo) * N_Y + y
    inter = (lo_grp, near, smp)
    intra = (lo_grp, seq, smp)
    y_up = lax.rem(y + 1, N_Y)
    y_down = lax.rem(y + N_Y - 1, N_Y)
    y_dev = ((lo * N_Y + y_up, seq, smp), (lo * N_Y + y_down, seq, smp))
    side = lax.rem((y + 1) // 2, 2)
    pair = (lo * N_Y + y + 1 - 2 * par, seq, smp)
    ext = (lo * N_Y + lax.rem(y + 2 * par + N_Y - 1, N_Y), seq, smp)
    core = lax.rem(smp, 2)
    x_up = lax.rem(smp // 2 + 1, N_X) * 2 + core
    x_down = lax.rem(smp // 2 + N_X - 1, N_X) * 2 + core
    x_far = lax.rem(smp // 2 + 2, N_X) * 2 + core
    x_dev = ((grp, seq, x_up), (grp, seq, x_down))
    core_dev = (grp, seq, smp + 1 - 2 * core)
    seq_dev = ((grp, up, smp), (grp, down, smp))

    native = pl.ds(pl.multiple_of(seq * depth, 16), depth)
    for c in range(chunks):
        p, part = c // SUBS, pl.ds(c % SUBS * depth, depth)
        if p == 0:
            for n, ref in enumerate((wk_ref, wv_ref)):
                pltpu.make_async_copy(
                    ref.at[part], w.at[c, native, pl.ds(n * HD, HD)], load_sem.at[0]
                ).start()
        else:
            col = pl.multiple_of((side * shared + 2 * p - 2) * HD, HD)
            pltpu.make_async_copy(
                wq_ref.at[part, pl.ds(col, PAIR)], w.at[c, native], load_sem.at[1]
            ).start()
    x_loads = [
        pltpu.make_async_copy(sx_ref, sxb, x_sem.at[0]),
        pltpu.make_async_copy(qg_ref, gains.at[1], x_sem.at[1]),
        pltpu.make_async_copy(kg_ref, gains.at[0], x_sem.at[1]),
    ]
    for sub in range(SUBS):
        for j in range(N_SEQ):
            x_loads.append(
                pltpu.make_async_copy(
                    px_ref.at[:, pl.ds((j * SUBS + sub) * depth, depth)],
                    xb.at[pl.ds(0, rows), pl.ds(sub * width + j * depth, depth)],
                    x_sem.at[2],
                )
            )
    for load in x_loads:
        load.start()

    barrier = pltpu.get_barrier_semaphore()
    for dev in (inter, intra) + y_dev + seq_dev:
        pl.semaphore_signal(barrier, inc=1, device_id=dev, device_id_type=MESH)
    for d in range(1, N_SMP):
        for s in (seq, mirror):
            pl.semaphore_signal(
                barrier, inc=1, device_id=(grp, s, lax.rem(smp + d, N_SMP)), device_id_type=MESH
            )
    pl.semaphore_wait(barrier, 6 + 2 * (N_SMP - 1))

    def message(c, kind, block, start, size, dev):
        ref = w.at[c, pl.ds(pl.multiple_of(block * depth + start, 16), size)]
        return pltpu.make_async_remote_copy(
            src_ref=ref, dst_ref=ref, send_sem=send_sem.at[kind], recv_sem=recv_sem.at[c, kind],
            device_id=dev, device_id_type=MESH,
        )

    mine = par * half
    theirs = (1 - par) * half

    def send_i1(c):
        for n, (first, last) in enumerate(((0, SUBS), (SUBS, chunks))):
            @pl.when(c == first)
            def _(n=n, first=first, last=last):
                ref = w.at[pl.ds(first, last - first), native]
                pltpu.make_async_copy(ref, ref, load_sem.at[n]).wait()

        message(c, I1, seq, mine, half, inter).start()

    def send_y(c, block, q):
        start = mine + q * quarter

        @pl.when(c < SUBS)
        def _():
            for n in range(2):
                @pl.when(q == n)
                def _():
                    message(c, Y, block, start, quarter, y_dev[n]).start()

        @pl.when(c >= SUBS)
        def _():
            message(c, Y, block, start, quarter, ext).start()

    def arrived(c, kind, block, start, size):
        message(c, kind, block, start, size, inter).wait_recv()

    for c in range(WINDOW):
        send_i1(chunk_at(jnp.int32(c)))

    rblock = count // X_CUTS
    share = SUBS * width // N_SMP

    core_sem = 4 * X_CUTS

    def x_message(n, buf, m, r, dev):
        at = (pl.ds(r * rblock, rblock), pl.ds(pl.multiple_of(m * share, HD), share))
        return pltpu.make_async_remote_copy(
            src_ref=buf.at[at], dst_ref=xp.at[at], send_sem=xs_send, recv_sem=xs_recv.at[n],
            device_id=dev, device_id_type=MESH,
        )

    def x_pair(r):
        return x_message(r, xb, smp, r, pair)

    def x_ring(way, r):
        return x_message((1 + way) * X_CUTS + r, xp, smp, r, x_dev[way])

    def x_fwd(way, r):
        return x_message(3 * X_CUTS + r, xp, (x_down, x_up)[way], r, x_dev[way])

    def x_core(k, r):
        return x_message(core_sem, xp, (smp, x_down, x_up, x_far)[k], r, core_dev)

    def x_step(n):
        stage, r = n // X_CUTS, n % X_CUTS
        if stage == 0:
            x_pair(r).wait_recv()
            x_ring(0, r).start()
            x_ring(1, r).start()
            x_core(0, r).start()
        elif stage == 1:
            for way in range(2):
                x_ring(way, r).wait_recv()
                if r // 2 == way:
                    x_fwd(way, r).start()
                x_core(1 + way, r).start()
        else:
            for way in range(2):
                x_fwd(way, 2 * way + r).wait_recv()
                x_core(3, 2 * way + r).start()

    def x_finish():
        ref = xp.at[:, pl.ds(0, N_X * share)]
        pltpu.make_async_copy(ref, ref, xs_recv.at[core_sem]).wait()

    def x_sent():
        pltpu.make_async_copy(xp, xp, xs_send).wait()

    def start_x():
        for n, ref in enumerate((sxb, gains, xb.at[pl.ds(0, rows)])):
            pltpu.make_async_copy(ref, ref, x_sem.at[n]).wait()
        for sub in range(SUBS):
            for j in range(N_SEQ):
                cols = (j * SUBS + sub) * depth
                at = sub * width + j * depth
                xb[rows:, at : at + depth] = sxb[:, :, cols : cols + depth].reshape(drows, depth)

    def prepare():
        row = lax.broadcasted_iota(jnp.int32, (count, HD), 0)
        lane = lax.broadcasted_iota(jnp.int32, (count, HD), 1)
        index = lax.rem(lane, HD // 2).astype(jnp.float32)
        freq = jnp.exp(index * (-2.0 * math.log(1e6) / HD))
        position = jnp.where(row < rows, seq * rows + row, N_SEQ * rows + lax.rem(row - rows, 4))
        angle = position.astype(jnp.float32) * freq
        cosine = jnp.cos(angle)
        sine = jnp.sin(angle)
        sine = jnp.where(lane < HD // 2, -sine, sine)
        fold = HD ** (-0.5) * math.log2(math.e)
        for n, factor in enumerate((1.0, fold)):
            gain = gains[n] * factor
            tabs[n, 0] = cosine * gain
            tabs[n, 1] = sine * pltpu.roll(gain, HD // 2, 1)
        vaug[:, :, HD:] = jnp.ones((N_SEQ, rows, HD), jnp.bfloat16)
        kvd[1, :, HD:] = jnp.ones((drows, HD), jnp.bfloat16)

    def rotated(n, u):
        r = lax.rsqrt(jnp.mean(u * u, -1, keepdims=True) + 1e-6)
        return (r * (u * tabs[n, 0] + pltpu.roll(u, HD // 2, 1) * tabs[n, 1])).astype(jnp.bfloat16)

    def kv_message(n, src, dev):
        return pltpu.make_async_remote_copy(
            src_ref=src, dst_ref=src, send_sem=kv_send, recv_sem=kv_recv.at[n], device_id=dev, device_id_type=MESH
        )

    def kv_own(part, way):
        return kv_message(0, kvx.at[seq, part], seq_dev[way])

    def kv_far(part):
        return kv_message(1, kvx.at[(down, up)[part], part], seq_dev[part])

    def kv_wait(n, blocks):
        ref = kvx.at[pl.ds(0, blocks)]
        pltpu.make_async_copy(ref, ref, (kv_recv.at[0], kv_recv.at[1], kv_send)[n]).wait()

    def out_copy(h):
        return pltpu.make_async_copy(
            obuf.at[h], out_ref.at[:, pl.ds(pl.multiple_of(h * HD, HD), HD)], o_sem
        )

    tile = rows // 2

    def attend_blocks(h, full):
        for r in range(2):
            q = qbuf[h, pl.ds(r * tile, tile)]
            e = jnp.exp2(dot_t(q, kvx[full, 0, pl.ds(r * tile, tile)]))
            allowed = lax.broadcasted_iota(jnp.int32, (tile, tile), 1) <= lax.broadcasted_iota(
                jnp.int32, (tile, tile), 0
            )
            e = jnp.where(allowed, e, 0.0).astype(jnp.bfloat16)
            total = dot(e, vaug[full, pl.ds(r * tile, tile)])
            if r > 0:
                e = jnp.exp2(dot_t(q, kvx[full, 0, pl.ds(0, tile)])).astype(jnp.bfloat16)
                total += dot(e, vaug[full, pl.ds(0, tile)])
            for j in range(full):
                e = jnp.exp2(dot_t(q, kvx[j, 0])).astype(jnp.bfloat16)
                total += dot(e, vaug[j])
            obuf[h, pl.ds(r * tile, tile)] = (total[:, :HD] / total[:, HD:]).astype(jnp.bfloat16)

    def attend_samples(h):
        q = qbuf[h, pl.ds(rows, drows)]
        a = lax.broadcasted_iota(jnp.int32, (drows, drows), 0)
        b = lax.broadcasted_iota(jnp.int32, (drows, drows), 1)
        own = jnp.where((b <= a) & (a // 4 == b // 4), jnp.exp2(dot_t(q, kvd[0, :, :HD])), 0.0)
        total = dot(own.astype(jnp.bfloat16), kvd[1])
        for j in range(N_SEQ):
            total += dot(jnp.exp2(dot_t(q, kvx[j, 0])).astype(jnp.bfloat16), vaug[j])
        res = total[:, :HD] / total[:, HD:]
        dsend[:, :, pl.ds(pl.multiple_of(h * HD, HD), HD)] = res.reshape(N_SMP, drows // N_SMP, HD)

    def attend(h):
        for full in range(N_SEQ):
            @pl.when(seq == full)
            def _(full=full):
                attend_blocks(h, full)

        out_copy(h).start()

    cols = heads * HD

    def d_message(g, n, to_seq, target):
        first = jnp.where(g < shared // 2, side, 1 - side) * shared + lax.rem(g, shared // 2) * 2
        col = pl.multiple_of(first * HD, HD)
        return pltpu.make_async_remote_copy(
            src_ref=dsend.at[target, :, pl.ds(col, PAIR)],
            dst_ref=dec_ref.at[:, pl.ds(pl.multiple_of(smp * cols + col, HD), PAIR)],
            send_sem=d_send.at[n], recv_sem=d_recv.at[n],
            device_id=(grp, to_seq, target), device_id_type=MESH,
        )

    def q_message(j):
        return pltpu.make_async_remote_copy(
            src_ref=qsend.at[j], dst_ref=qbuf.at[side * shared + j], send_sem=q_send, recv_sem=q_recv.at[j],
            device_id=pair, device_id_type=MESH,
        )

    def x_cols(sub):
        return pl.ds(pl.multiple_of(sub * width, HD), width)

    def accumulate(ref, x_ref, c):
        sub = lax.rem(c, SUBS)
        part = dot(x_ref[:, x_cols(sub)], w[c])

        @pl.when(sub == 0)
        def _():
            ref[...] = part

        @pl.when(sub > 0)
        def _():
            ref[...] += part

    def partner(n, _):
        accumulate(projp, xp, SUBS + n)

        @pl.when(lax.rem(n, SUBS) == SUBS - 1)
        def _():
            for k in range(2):
                j = n // SUBS * 2 + k
                qsend[j] = rotated(1, projp[:, k * HD : (k + 1) * HD])
                q_message(j).start()

        return 0

    def one(n, _):
        g = n // 2
        received = g >= shared // 2
        j = lax.rem(g, shared // 2) * 2
        first = jnp.where(received, 1 - side, side) * shared + j
        opening = lax.rem(n, 2) == 0

        @pl.when(opening & received)
        def _():
            q_message(j).wait_recv()
            q_message(j + 1).wait_recv()

        @pl.when(opening & ((seq < N_SEQ // 2) | (g == shared - 1)))
        def _():
            attend_samples(first)
            attend_samples(first + 1)
            for d in range(1, N_SMP):
                d_message(g, 0, seq, lax.rem(smp + d, N_SMP)).start()

        @pl.when(opening & (seq < N_SEQ // 2) & (g < shared - 1))
        def _():
            for d in range(N_SMP):
                d_message(g, 1, mirror, lax.rem(smp + d, N_SMP)).start()

        attend(first + lax.rem(n, 2))
        return 0

    def x_place(place):
        @pl.when((place >= min(X_STEPS)) & (place <= max(X_STEPS)))
        def _():
            for n, at in enumerate(X_STEPS):
                @pl.when(place == at)
                def _(n=n):
                    x_step(n)

    def step(i, _):
        t = chunk_at(i - LAG)
        new = chunk_at(i)

        @pl.when(i < chunks)
        def _():
            arrived(new, I1, near, mine, half)
            message(new, J1, near, mine, half, intra).start()
            for q in range(2):
                send_y(new, near, q)

        @pl.when(i + WINDOW < chunks)
        def _():
            send_i1(chunk_at(i + WINDOW))

        @pl.when(i == 0)
        def _():
            start_x()

        for n, at in enumerate(X_START):
            @pl.when(i == at)
            def _(n=n):
                x_pair(n).start()

        @pl.when((i >= AT_J1) & (i - AT_J1 < chunks))
        def _():
            c = chunk_at(i - AT_J1)
            arrived(c, J1, other, mine, half)
            message(c, I2, other, mine + (1 - lo) * quarter, quarter, inter).start()
            for q in range(2):
                send_y(c, other, q)

        x_place(2 * i)

        @pl.when((i >= AT_I2) & (i - AT_I2 < chunks))
        def _():
            c = chunk_at(i - AT_I2)
            arrived(c, I2, far, mine + lo * quarter, quarter)
            message(c, J2, far, mine + lo * quarter, quarter, intra).start()
            send_y(c, far, lo)

        @pl.when((i >= AT_J2) & (i - AT_J2 < chunks))
        def _():
            c = chunk_at(i - AT_J2)
            arrived(c, J2, far, mine + (1 - lo) * quarter, quarter)
            send_y(c, far, 1 - lo)

        @pl.when(i == 1)
        def _():
            prepare()

        @pl.when(i == KV_ON)
        def _():
            kv_wait(0, 2)
            for part in range(2):
                kv_far(part).start()

        active = i >= LAG

        @pl.when(active)
        def _():
            message(t, Y, 0, 0, 3 * half, inter).wait_recv()

        x_place(2 * i + 1)

        @pl.when(i == PARTNER_AT[0])
        def _():
            x_finish()

        lax.fori_loop(reached(i - 1, PARTNER_AT), reached(i, PARTNER_AT), partner, 0)

        @pl.when(active)
        def _():
            accumulate(proj.at[jnp.minimum(t // SUBS, 1)], xb, t)

            @pl.when(t == SUBS - 1)
            def _():
                k = rotated(0, proj[0, :, :HD])
                v = proj[0, :, HD:].astype(jnp.bfloat16)
                kvx[seq, 0] = k[:rows]
                kvx[seq, 1] = v[:rows]
                kvd[0, :, :HD] = k[rows:]
                kvd[1, :, :HD] = v[rows:]
                for part in range(2):
                    for way in range(2):
                        kv_own(part, way).start()

            @pl.when((t >= SUBS) & (lax.rem(t, SUBS) == SUBS - 1))
            def _():
                for k in range(2):
                    qbuf[side * shared + (t // SUBS - 1) * 2 + k] = rotated(1, proj[1, :, k * HD : (k + 1) * HD])

        @pl.when(i == KV_END)
        def _():
            kv_wait(1, 1)
            vaug[:, :, :HD] = kvx[:, 1]

        lax.fori_loop(reached(i - 1, ATTEND_AT), reached(i, ATTEND_AT), one, 0)
        return 0

    lax.fori_loop(0, chunks + LAG, step, 0)

    @pl.when(seq < N_SEQ // 2)
    def _():
        dec_ref[:, pl.ds(pl.multiple_of(smp * cols, HD), cols)] = dsend[smp]

    @pl.when(seq >= N_SEQ // 2)
    def _():
        col = pl.multiple_of((1 - side) * shared * HD + (shared - 2) * HD, HD)
        dec_ref[:, pl.ds(pl.multiple_of(smp * cols + col, HD), PAIR)] = dsend[smp, :, pl.ds(col, PAIR)]

    for kind, size in ((I1, half), (J1, half), (I2, quarter), (J2, quarter), (Y, 3 * half)):
        ref = w.at[:, pl.ds(0, size)]
        pltpu.make_async_remote_copy(
            src_ref=ref, dst_ref=ref, send_sem=send_sem.at[kind], recv_sem=recv_sem.at[0, kind],
            device_id=inter, device_id_type=MESH,
        ).wait_send()
    x_sent()
    pltpu.make_async_copy(qsend, qsend, q_send).wait()
    kv_wait(2, 3)
    pltpu.make_async_copy(obuf, obuf, o_sem).wait()

    early = dsend.at[:, :, pl.ds(0, cols - PAIR)]

    @pl.when(seq < N_SEQ // 2)
    def _():
        part = dsend.at[pl.ds(0, N_SMP - 1)]
        pltpu.make_async_copy(early, early, d_send.at[1]).wait()
        pltpu.make_async_copy(part, part, d_send.at[0]).wait()
        pltpu.make_async_copy(part, part, d_recv.at[0]).wait()

    @pl.when(seq >= N_SEQ // 2)
    def _():
        part = dsend.at[pl.ds(0, N_SMP - 1), :, pl.ds(0, PAIR)]
        pltpu.make_async_copy(part, part, d_send.at[0]).wait()
        pltpu.make_async_copy(early, early, d_recv.at[1]).wait()
        pltpu.make_async_copy(part, part, d_recv.at[0]).wait()

    dout_ref[...] = dec_ref[...].astype(jnp.bfloat16)


def local(prompt_x, sampled_x, w_query, w_key, w_value, q_gain, k_gain):
    rows, width = prompt_x.shape
    samples, steps, _ = sampled_x.shape
    drows = samples * steps
    q_cols = w_query.shape[1]
    heads = q_cols // HD
    shared = heads // 2
    chunks = SUBS * (1 + shared // 2)
    count = rows + drows
    mine = drows // N_SMP
    hbm = pl.BlockSpec(memory_space=pltpu.HBM)
    vmem = pl.BlockSpec(memory_space=pltpu.VMEM)
    dma = pltpu.SemaphoreType.DMA
    prefill, dec = pl.pallas_call(
        kernel,
        out_shape=(
            jax.ShapeDtypeStruct((rows, q_cols), jnp.bfloat16),
            jax.ShapeDtypeStruct((mine, N_SMP * q_cols), jnp.bfloat16),
        ),
        in_specs=[hbm] * 7,
        out_specs=(pl.BlockSpec(memory_space=pl.ANY), vmem),
        scratch_shapes=[
            pltpu.VMEM((count, width), jnp.bfloat16),
            pltpu.VMEM((count, width), jnp.bfloat16),
            pltpu.VMEM((samples, steps, width), jnp.bfloat16),
            pltpu.VMEM((chunks, width // SUBS, PAIR), jnp.bfloat16),
            pltpu.VMEM((2, count, PAIR), jnp.float32),
            pltpu.VMEM((count, PAIR), jnp.float32),
            pltpu.VMEM((shared, count, HD), jnp.bfloat16),
            pltpu.VMEM((2, 2, count, HD), jnp.float32),
            pltpu.VMEM((2, 1, HD), jnp.float32),
            pltpu.VMEM((N_SEQ, 2, rows, HD), jnp.bfloat16),
            pltpu.VMEM((N_SEQ, rows, PAIR), jnp.bfloat16),
            pltpu.VMEM((2, drows, PAIR), jnp.bfloat16),
            pltpu.VMEM((heads, count, HD), jnp.bfloat16),
            pltpu.VMEM((heads, rows, HD), jnp.bfloat16),
            pltpu.VMEM((N_SMP, mine, q_cols), jnp.float32),
            pltpu.VMEM((mine, N_SMP * q_cols), jnp.float32),
            dma((2,)),
            dma((3,)),
            dma,
            dma((5,)),
            dma((chunks, 5)),
            dma,
            dma((2,)),
            dma((2,)),
            dma((2,)),
            dma,
            dma((4 * X_CUTS + 1,)),
            dma,
            dma((shared,)),
        ],
        compiler_params=pltpu.CompilerParams(
            collective_id=0, has_side_effects=True, vmem_limit_bytes=58 * 2**20
        ),
    )(prompt_x, sampled_x, w_query, w_key, w_value, q_gain.reshape(1, HD), k_gain.reshape(1, HD))
    return prefill, dec.reshape(samples // N_SMP, steps, N_SMP * q_cols)


def solution(mesh):
    in_specs = (
        P(("grp", "seq"), None),
        P("grp", None, None),
        P("seq", "smp"),
        P("seq", "smp"),
        P("seq", "smp"),
        P(),
        P(),
    )
    out_specs = (P(("grp", "seq"), "smp"), P(("grp", "smp"), None, None))
    return jax.shard_map(local, mesh=mesh, in_specs=in_specs, out_specs=out_specs, check_vma=False)
```

```python
import math

import jax
import jax.numpy as jnp
from jax import lax
from jax.experimental import pallas as pl
from jax.experimental.pallas import tpu as pltpu
from jax.sharding import PartitionSpec as P

HD = 128
PAIR = 2 * HD
MESH = pl.DeviceIdType.MESH
N_Y = 4
N_SEQ = 4
N_SMP = 8
N_X = N_SMP // 2
SUBS = 5
X_CUTS = 4
WINDOW = 2
OUT_CUTS = 4
AT_J1 = 1
AT_I2 = 2
AT_J2 = 3
LAG = 5
KV_ON = 12
KV_END = 14
X_START = (3, 5, 7, 9)
X_STEPS = (11, 15, 19, 23, 16, 20, 24, 27, 28, 30)
PARTNER_AT = (15, 15, 16, 16, 16, 17, 17, 18, 18, 19)
ATTEND_AT = (19, 19, 19, 19, 19, 19, 19, 19)
I1, J1, I2, J2, Y = 0, 1, 2, 3, 4


def reached(i, steps):
    return sum((i >= step).astype(jnp.int32) for step in steps)


def chunk_at(i):
    return jnp.where((i < 3) | (i > 5), i, jnp.where(i == 3, SUBS, i - 1))


def dot(a, b):
    return jnp.dot(a, b, preferred_element_type=jnp.float32)


def dot_t(a, b):
    return lax.dot_general(a, b, (((1,), (1,)), ((), ())), preferred_element_type=jnp.float32)


def kernel(
    px_ref, sx_ref, wq_ref, wk_ref, wv_ref, qg_ref, kg_ref,
    out_ref, dout_ref,
    xb, xp, sxb, w, proj, projp, qsend, tabs, gains, kvx, vaug, kvd, qbuf, obuf, dsend, dec_ref,
    load_sem, x_sem, o_sem, send_sem, recv_sem, kv_send, kv_recv, d_send, d_recv, xs_send, xs_recv, q_send, q_recv,
):
    rows = px_ref.shape[0]
    drows = sx_ref.shape[0] * sx_ref.shape[1]
    heads = wq_ref.shape[1] // HD
    shared = heads // 2
    depth = wq_ref.shape[0] // SUBS
    width = N_SEQ * depth
    chunks = SUBS * (1 + shared // 2)
    count = rows + drows
    half = depth // 2
    quarter = depth // 4
    grp = lax.axis_index("grp")
    seq = lax.axis_index("seq")
    smp = lax.axis_index("smp")
    lo = grp // N_Y
    y = lax.rem(grp, N_Y)
    par = lax.rem(y, 2)
    up = lax.rem(seq + 1, N_SEQ)
    down = lax.rem(seq + N_SEQ - 1, N_SEQ)
    far = lax.rem(seq + 2, N_SEQ)
    mirror = N_SEQ - 1 - seq
    near = lax.rem(seq + 2 * lo + N_SEQ - 1, N_SEQ)
    other = lax.rem(seq + N_SEQ + 1 - 2 * lo, N_SEQ)
    lo_grp = (1 - lo) * N_Y + y
    inter = (lo_grp, near, smp)
    intra = (lo_grp, seq, smp)
    y_up = lax.rem(y + 1, N_Y)
    y_down = lax.rem(y + N_Y - 1, N_Y)
    y_dev = ((lo * N_Y + y_up, seq, smp), (lo * N_Y + y_down, seq, smp))
    side = lax.rem((y + 1) // 2, 2)
    pair = (lo * N_Y + y + 1 - 2 * par, seq, smp)
    ext = (lo * N_Y + lax.rem(y + 2 * par + N_Y - 1, N_Y), seq, smp)
    core = lax.rem(smp, 2)
    x_up = lax.rem(smp // 2 + 1, N_X) * 2 + core
    x_down = lax.rem(smp // 2 + N_X - 1, N_X) * 2 + core
    x_far = lax.rem(smp // 2 + 2, N_X) * 2 + core
    x_dev = ((grp, seq, x_up), (grp, seq, x_down))
    core_dev = (grp, seq, smp + 1 - 2 * core)
    seq_dev = ((grp, up, smp), (grp, down, smp))

    native = pl.ds(pl.multiple_of(seq * depth, 16), depth)
    for c in range(chunks):
        p, part = c // SUBS, pl.ds(c % SUBS * depth, depth)
        if p == 0:
            for n, ref in enumerate((wk_ref, wv_ref)):
                pltpu.make_async_copy(
                    ref.at[part], w.at[c, native, pl.ds(n * HD, HD)], load_sem.at[0]
                ).start()
        else:
            col = pl.multiple_of((side * shared + 2 * p - 2) * HD, HD)
            pltpu.make_async_copy(
                wq_ref.at[part, pl.ds(col, PAIR)], w.at[c, native], load_sem.at[1]
            ).start()
    x_loads = [
        pltpu.make_async_copy(sx_ref, sxb, x_sem.at[0]),
        pltpu.make_async_copy(qg_ref, gains.at[1], x_sem.at[1]),
        pltpu.make_async_copy(kg_ref, gains.at[0], x_sem.at[1]),
    ]
    for sub in range(SUBS):
        for j in range(N_SEQ):
            x_loads.append(
                pltpu.make_async_copy(
                    px_ref.at[:, pl.ds((j * SUBS + sub) * depth, depth)],
                    xb.at[pl.ds(0, rows), pl.ds(sub * width + j * depth, depth)],
                    x_sem.at[2],
                )
            )
    for load in x_loads:
        load.start()

    barrier = pltpu.get_barrier_semaphore()
    for dev in (inter, intra) + y_dev + seq_dev:
        pl.semaphore_signal(barrier, inc=1, device_id=dev, device_id_type=MESH)
    for d in range(1, N_SMP):
        for s in (seq, mirror):
            pl.semaphore_signal(
                barrier, inc=1, device_id=(grp, s, lax.rem(smp + d, N_SMP)), device_id_type=MESH
            )
    pl.semaphore_wait(barrier, 6 + 2 * (N_SMP - 1))

    def message(c, kind, block, start, size, dev):
        ref = w.at[c, pl.ds(pl.multiple_of(block * depth + start, 16), size)]
        return pltpu.make_async_remote_copy(
            src_ref=ref, dst_ref=ref, send_sem=send_sem.at[kind], recv_sem=recv_sem.at[c, kind],
            device_id=dev, device_id_type=MESH,
        )

    mine = par * half
    theirs = (1 - par) * half

    def send_i1(c):
        for n, (first, last) in enumerate(((0, SUBS), (SUBS, chunks))):
            @pl.when(c == first)
            def _(n=n, first=first, last=last):
                ref = w.at[pl.ds(first, last - first), native]
                pltpu.make_async_copy(ref, ref, load_sem.at[n]).wait()

        message(c, I1, seq, mine, half, inter).start()

    def send_y(c, block, q):
        start = mine + q * quarter

        @pl.when(c < SUBS)
        def _():
            for n in range(2):
                @pl.when(q == n)
                def _():
                    message(c, Y, block, start, quarter, y_dev[n]).start()

        @pl.when(c >= SUBS)
        def _():
            message(c, Y, block, start, quarter, ext).start()

    def arrived(c, kind, block, start, size):
        message(c, kind, block, start, size, inter).wait_recv()

    for c in range(WINDOW):
        send_i1(chunk_at(jnp.int32(c)))

    rblock = count // X_CUTS
    share = SUBS * width // N_SMP

    core_sem = 4 * X_CUTS

    def x_message(n, buf, m, r, dev):
        at = (pl.ds(r * rblock, rblock), pl.ds(pl.multiple_of(m * share, HD), share))
        return pltpu.make_async_remote_copy(
            src_ref=buf.at[at], dst_ref=xp.at[at], send_sem=xs_send, recv_sem=xs_recv.at[n],
            device_id=dev, device_id_type=MESH,
        )

    def x_pair(r):
        return x_message(r, xb, smp, r, pair)

    def x_ring(way, r):
        return x_message((1 + way) * X_CUTS + r, xp, smp, r, x_dev[way])

    def x_fwd(way, r):
        return x_message(3 * X_CUTS + r, xp, (x_down, x_up)[way], r, x_dev[way])

    def x_core(k, r):
        return x_message(core_sem, xp, (smp, x_down, x_up, x_far)[k], r, core_dev)

    def x_step(n):
        stage, r = n // X_CUTS, n % X_CUTS
        if stage == 0:
            x_pair(r).wait_recv()
            x_ring(0, r).start()
            x_ring(1, r).start()
            x_core(0, r).start()
        elif stage == 1:
            for way in range(2):
                x_ring(way, r).wait_recv()
                if r // 2 == way:
                    x_fwd(way, r).start()
                x_core(1 + way, r).start()
        else:
            for way in range(2):
                x_fwd(way, 2 * way + r).wait_recv()
                x_core(3, 2 * way + r).start()

    def x_finish():
        ref = xp.at[:, pl.ds(0, N_X * share)]
        pltpu.make_async_copy(ref, ref, xs_recv.at[core_sem]).wait()

    def x_sent():
        pltpu.make_async_copy(xp, xp, xs_send).wait()

    def start_x():
        for n, ref in enumerate((sxb, gains, xb.at[pl.ds(0, rows)])):
            pltpu.make_async_copy(ref, ref, x_sem.at[n]).wait()
        for sub in range(SUBS):
            for j in range(N_SEQ):
                cols = (j * SUBS + sub) * depth
                at = sub * width + j * depth
                xb[rows:, at : at + depth] = sxb[:, :, cols : cols + depth].reshape(drows, depth)

    def prepare():
        row = lax.broadcasted_iota(jnp.int32, (count, HD), 0)
        lane = lax.broadcasted_iota(jnp.int32, (count, HD), 1)
        index = lax.rem(lane, HD // 2).astype(jnp.float32)
        freq = jnp.exp(index * (-2.0 * math.log(1e6) / HD))
        position = jnp.where(row < rows, seq * rows + row, N_SEQ * rows + lax.rem(row - rows, 4))
        angle = position.astype(jnp.float32) * freq
        cosine = jnp.cos(angle)
        sine = jnp.sin(angle)
        sine = jnp.where(lane < HD // 2, -sine, sine)
        fold = HD ** (-0.5) * math.log2(math.e)
        for n, factor in enumerate((1.0, fold)):
            gain = gains[n] * factor
            tabs[n, 0] = cosine * gain
            tabs[n, 1] = sine * pltpu.roll(gain, HD // 2, 1)
        vaug[:, :, HD:] = jnp.ones((N_SEQ, rows, HD), jnp.bfloat16)
        kvd[1, :, HD:] = jnp.ones((drows, HD), jnp.bfloat16)

    def rotated(n, u):
        r = lax.rsqrt(jnp.mean(u * u, -1, keepdims=True) + 1e-6)
        return (r * (u * tabs[n, 0] + pltpu.roll(u, HD // 2, 1) * tabs[n, 1])).astype(jnp.bfloat16)

    def kv_message(n, src, dev):
        return pltpu.make_async_remote_copy(
            src_ref=src, dst_ref=src, send_sem=kv_send, recv_sem=kv_recv.at[n], device_id=dev, device_id_type=MESH
        )

    def kv_own(part, way):
        return kv_message(0, kvx.at[seq, part], seq_dev[way])

    def kv_far(part):
        return kv_message(1, kvx.at[(down, up)[part], part], seq_dev[part])

    def kv_wait(n, blocks):
        ref = kvx.at[pl.ds(0, blocks)]
        pltpu.make_async_copy(ref, ref, (kv_recv.at[0], kv_recv.at[1], kv_send)[n]).wait()

    def out_copy(h):
        return pltpu.make_async_copy(
            obuf.at[h], out_ref.at[:, pl.ds(pl.multiple_of(h * HD, HD), HD)], o_sem
        )

    tile = rows // 2

    def attend_blocks(h, full):
        for r in range(2):
            q = qbuf[h, pl.ds(r * tile, tile)]
            e = jnp.exp2(dot_t(q, kvx[full, 0, pl.ds(r * tile, tile)]))
            allowed = lax.broadcasted_iota(jnp.int32, (tile, tile), 1) <= lax.broadcasted_iota(
                jnp.int32, (tile, tile), 0
            )
            e = jnp.where(allowed, e, 0.0).astype(jnp.bfloat16)
            total = dot(e, vaug[full, pl.ds(r * tile, tile)])
            if r > 0:
                e = jnp.exp2(dot_t(q, kvx[full, 0, pl.ds(0, tile)])).astype(jnp.bfloat16)
                total += dot(e, vaug[full, pl.ds(0, tile)])
            for j in range(full):
                e = jnp.exp2(dot_t(q, kvx[j, 0])).astype(jnp.bfloat16)
                total += dot(e, vaug[j])
            obuf[h, pl.ds(r * tile, tile)] = (total[:, :HD] / total[:, HD:]).astype(jnp.bfloat16)

    def attend_samples(h):
        q = qbuf[h, pl.ds(rows, drows)]
        a = lax.broadcasted_iota(jnp.int32, (drows, drows), 0)
        b = lax.broadcasted_iota(jnp.int32, (drows, drows), 1)
        own = jnp.where((b <= a) & (a // 4 == b // 4), jnp.exp2(dot_t(q, kvd[0, :, :HD])), 0.0)
        total = dot(own.astype(jnp.bfloat16), kvd[1])
        for j in range(N_SEQ):
            total += dot(jnp.exp2(dot_t(q, kvx[j, 0])).astype(jnp.bfloat16), vaug[j])
        res = total[:, :HD] / total[:, HD:]
        dsend[:, :, :, pl.ds(pl.multiple_of(h * HD, HD), HD)] = res.reshape(dsend.shape[:3] + (HD,))

    def attend(h):
        for full in range(N_SEQ):
            @pl.when(seq == full)
            def _(full=full):
                attend_blocks(h, full)

        out_copy(h).start()

    cols = heads * HD

    def d_message(g, n, to_seq, target):
        first = jnp.where(g < shared // 2, side, 1 - side) * shared + lax.rem(g, shared // 2) * 2
        col = pl.multiple_of(first * HD, HD)
        return pltpu.make_async_remote_copy(
            src_ref=dsend.at[target, :, :, pl.ds(col, PAIR)],
            dst_ref=dec_ref.at[:, :, pl.ds(pl.multiple_of(smp * cols + col, HD), PAIR)],
            send_sem=d_send.at[n], recv_sem=d_recv.at[n],
            device_id=(grp, to_seq, target), device_id_type=MESH,
        )

    def q_message(j):
        return pltpu.make_async_remote_copy(
            src_ref=qsend.at[j], dst_ref=qbuf.at[side * shared + j], send_sem=q_send, recv_sem=q_recv.at[j],
            device_id=pair, device_id_type=MESH,
        )

    def x_cols(sub):
        return pl.ds(pl.multiple_of(sub * width, HD), width)

    def accumulate(ref, x_ref, c):
        sub = lax.rem(c, SUBS)
        part = dot(x_ref[:, x_cols(sub)], w[c])

        @pl.when(sub == 0)
        def _():
            ref[...] = part

        @pl.when(sub > 0)
        def _():
            ref[...] += part

    def partner(n, _):
        accumulate(projp, xp, SUBS + n)

        @pl.when(lax.rem(n, SUBS) == SUBS - 1)
        def _():
            for k in range(2):
                j = n // SUBS * 2 + k
                qsend[j] = rotated(1, projp[:, k * HD : (k + 1) * HD])
                q_message(j).start()

        return 0

    def one(n, _):
        g = n // 2
        received = g >= shared // 2
        j = lax.rem(g, shared // 2) * 2
        first = jnp.where(received, 1 - side, side) * shared + j
        opening = lax.rem(n, 2) == 0

        @pl.when(opening & received)
        def _():
            q_message(j).wait_recv()
            q_message(j + 1).wait_recv()

        @pl.when(opening & ((seq < N_SEQ // 2) | (g == shared - 1)))
        def _():
            attend_samples(first)
            attend_samples(first + 1)
            for d in range(1, N_SMP):
                d_message(g, 0, seq, lax.rem(smp + d, N_SMP)).start()

        @pl.when(opening & (seq < N_SEQ // 2) & (g < shared - 1))
        def _():
            for d in range(N_SMP):
                d_message(g, 1, mirror, lax.rem(smp + d, N_SMP)).start()

        attend(first + lax.rem(n, 2))
        return 0

    def x_place(place):
        @pl.when((place >= min(X_STEPS)) & (place <= max(X_STEPS)))
        def _():
            for n, at in enumerate(X_STEPS):
                @pl.when(place == at)
                def _(n=n):
                    x_step(n)

    def step(i, _):
        t = chunk_at(i - LAG)
        new = chunk_at(i)

        @pl.when(i < chunks)
        def _():
            arrived(new, I1, near, mine, half)
            message(new, J1, near, mine, half, intra).start()
            for q in range(2):
                send_y(new, near, q)

        @pl.when(i + WINDOW < chunks)
        def _():
            send_i1(chunk_at(i + WINDOW))

        @pl.when(i == 0)
        def _():
            start_x()

        for n, at in enumerate(X_START):
            @pl.when(i == at)
            def _(n=n):
                x_pair(n).start()

        @pl.when((i >= AT_J1) & (i - AT_J1 < chunks))
        def _():
            c = chunk_at(i - AT_J1)
            arrived(c, J1, other, mine, half)
            message(c, I2, other, mine + (1 - lo) * quarter, quarter, inter).start()
            for q in range(2):
                send_y(c, other, q)

        x_place(2 * i)

        @pl.when((i >= AT_I2) & (i - AT_I2 < chunks))
        def _():
            c = chunk_at(i - AT_I2)
            arrived(c, I2, far, mine + lo * quarter, quarter)
            message(c, J2, far, mine + lo * quarter, quarter, intra).start()
            send_y(c, far, lo)

        @pl.when((i >= AT_J2) & (i - AT_J2 < chunks))
        def _():
            c = chunk_at(i - AT_J2)
            arrived(c, J2, far, mine + (1 - lo) * quarter, quarter)
            send_y(c, far, 1 - lo)

        @pl.when(i == 1)
        def _():
            prepare()

        @pl.when(i == KV_ON)
        def _():
            kv_wait(0, 2)
            for part in range(2):
                kv_far(part).start()

        active = i >= LAG

        @pl.when(active)
        def _():
            message(t, Y, 0, 0, 3 * half, inter).wait_recv()

        x_place(2 * i + 1)

        @pl.when(i == PARTNER_AT[0])
        def _():
            x_finish()

        lax.fori_loop(reached(i - 1, PARTNER_AT), reached(i, PARTNER_AT), partner, 0)

        @pl.when(active)
        def _():
            accumulate(proj.at[jnp.minimum(t // SUBS, 1)], xb, t)

            @pl.when(t == SUBS - 1)
            def _():
                k = rotated(0, proj[0, :, :HD])
                v = proj[0, :, HD:].astype(jnp.bfloat16)
                kvx[seq, 0] = k[:rows]
                kvx[seq, 1] = v[:rows]
                kvd[0, :, :HD] = k[rows:]
                kvd[1, :, :HD] = v[rows:]
                for part in range(2):
                    for way in range(2):
                        kv_own(part, way).start()

            @pl.when((t >= SUBS) & (lax.rem(t, SUBS) == SUBS - 1))
            def _():
                for k in range(2):
                    qbuf[side * shared + (t // SUBS - 1) * 2 + k] = rotated(1, proj[1, :, k * HD : (k + 1) * HD])

        @pl.when(i == KV_END)
        def _():
            kv_wait(1, 1)
            vaug[:, :, :HD] = kvx[:, 1]

        lax.fori_loop(reached(i - 1, ATTEND_AT), reached(i, ATTEND_AT), one, 0)
        return 0

    lax.fori_loop(0, chunks + LAG, step, 0)

    @pl.when(seq < N_SEQ // 2)
    def _():
        dec_ref[:, :, pl.ds(pl.multiple_of(smp * cols, HD), cols)] = dsend[smp]

    @pl.when(seq >= N_SEQ // 2)
    def _():
        col = pl.multiple_of((1 - side) * shared * HD + (shared - 2) * HD, HD)
        dec_ref[:, :, pl.ds(pl.multiple_of(smp * cols + col, HD), PAIR)] = dsend[smp, :, :, pl.ds(col, PAIR)]

    for kind, size in ((I1, half), (J1, half), (I2, quarter), (J2, quarter), (Y, 3 * half)):
        ref = w.at[:, pl.ds(0, size)]
        pltpu.make_async_remote_copy(
            src_ref=ref, dst_ref=ref, send_sem=send_sem.at[kind], recv_sem=recv_sem.at[0, kind],
            device_id=inter, device_id_type=MESH,
        ).wait_send()
    x_sent()
    pltpu.make_async_copy(qsend, qsend, q_send).wait()
    kv_wait(2, 3)
    pltpu.make_async_copy(obuf, obuf, o_sem).wait()

    early = dsend.at[:, :, :, pl.ds(0, cols - PAIR)]

    @pl.when(seq < N_SEQ // 2)
    def _():
        part = dsend.at[pl.ds(0, N_SMP - 1)]
        pltpu.make_async_copy(early, early, d_send.at[1]).wait()
        pltpu.make_async_copy(part, part, d_send.at[0]).wait()
        pltpu.make_async_copy(part, part, d_recv.at[0]).wait()

    @pl.when(seq >= N_SEQ // 2)
    def _():
        part = dsend.at[pl.ds(0, N_SMP - 1), :, :, pl.ds(0, PAIR)]
        pltpu.make_async_copy(part, part, d_send.at[0]).wait()
        pltpu.make_async_copy(early, early, d_recv.at[1]).wait()
        pltpu.make_async_copy(part, part, d_recv.at[0]).wait()

    dout_ref[...] = dec_ref[...].astype(jnp.bfloat16)


def deliver(p_ref, d_ref, out_ref, dec_ref, p_buf, d_buf, sem):
    size = p_ref.shape[0] // OUT_CUTS
    ways = [(d_ref, d_buf, dec_ref)]
    for n in range(OUT_CUTS):
        ways.append(tuple(ref.at[pl.ds(n * size, size)] for ref in (p_ref, p_buf, out_ref)))
    for n, (src, buf, _) in enumerate(ways):
        pltpu.make_async_copy(src, buf, sem.at[0, n]).start()
    for n, (src, buf, dst) in enumerate(ways):
        pltpu.make_async_copy(src, buf, sem.at[0, n]).wait()
        pltpu.make_async_copy(buf, dst, sem.at[1, n]).start()
    for n, (_, buf, dst) in enumerate(ways):
        pltpu.make_async_copy(buf, dst, sem.at[1, n]).wait()


def local(prompt_x, sampled_x, w_query, w_key, w_value, q_gain, k_gain):
    rows, width = prompt_x.shape
    samples, steps, _ = sampled_x.shape
    drows = samples * steps
    q_cols = w_query.shape[1]
    heads = q_cols // HD
    shared = heads // 2
    chunks = SUBS * (1 + shared // 2)
    count = rows + drows
    own = samples // N_SMP
    hbm = pl.BlockSpec(memory_space=pltpu.HBM)
    vmem = pl.BlockSpec(memory_space=pltpu.VMEM)
    dma = pltpu.SemaphoreType.DMA
    prefill, dec = pl.pallas_call(
        kernel,
        out_shape=(
            jax.ShapeDtypeStruct((rows, q_cols), jnp.bfloat16),
            jax.ShapeDtypeStruct((own, steps, N_SMP * q_cols), jnp.bfloat16),
        ),
        in_specs=[hbm] * 7,
        out_specs=(pl.BlockSpec(memory_space=pl.ANY), vmem),
        scratch_shapes=[
            pltpu.VMEM((count, width), jnp.bfloat16),
            pltpu.VMEM((count, width), jnp.bfloat16),
            pltpu.VMEM((samples, steps, width), jnp.bfloat16),
            pltpu.VMEM((chunks, width // SUBS, PAIR), jnp.bfloat16),
            pltpu.VMEM((2, count, PAIR), jnp.float32),
            pltpu.VMEM((count, PAIR), jnp.float32),
            pltpu.VMEM((shared, count, HD), jnp.bfloat16),
            pltpu.VMEM((2, 2, count, HD), jnp.float32),
            pltpu.VMEM((2, 1, HD), jnp.float32),
            pltpu.VMEM((N_SEQ, 2, rows, HD), jnp.bfloat16),
            pltpu.VMEM((N_SEQ, rows, PAIR), jnp.bfloat16),
            pltpu.VMEM((2, drows, PAIR), jnp.bfloat16),
            pltpu.VMEM((heads, count, HD), jnp.bfloat16),
            pltpu.VMEM((heads, rows, HD), jnp.bfloat16),
            pltpu.VMEM((N_SMP, own, steps, q_cols), jnp.float32),
            pltpu.VMEM((own, steps, N_SMP * q_cols), jnp.float32),
            dma((2,)),
            dma((3,)),
            dma,
            dma((5,)),
            dma((chunks, 5)),
            dma,
            dma((2,)),
            dma((2,)),
            dma((2,)),
            dma,
            dma((4 * X_CUTS + 1,)),
            dma,
            dma((shared,)),
        ],
        compiler_params=pltpu.CompilerParams(
            collective_id=0, has_side_effects=True, vmem_limit_bytes=58 * 2**20
        ),
    )(prompt_x, sampled_x, w_query, w_key, w_value, q_gain.reshape(1, HD), k_gain.reshape(1, HD))
    return pl.pallas_call(
        deliver,
        out_shape=(
            jax.ShapeDtypeStruct((rows, q_cols), jnp.bfloat16),
            jax.ShapeDtypeStruct((own, steps, N_SMP * q_cols), jnp.bfloat16),
        ),
        in_specs=[hbm, hbm],
        out_specs=(hbm, hbm),
        scratch_shapes=[
            pltpu.VMEM((rows, q_cols), jnp.bfloat16),
            pltpu.VMEM((own, steps, N_SMP * q_cols), jnp.bfloat16),
            dma((2, 1 + OUT_CUTS)),
        ],
        compiler_params=pltpu.CompilerParams(vmem_limit_bytes=58 * 2**20),
    )(prefill, dec)


def solution(mesh):
    in_specs = (
        P(("grp", "seq"), None),
        P("grp", None, None),
        P("seq", "smp"),
        P("seq", "smp"),
        P("seq", "smp"),
        P(),
        P(),
    )
    out_specs = (P(("grp", "seq"), "smp"), P(("grp", "smp"), None, None))
    return jax.shard_map(local, mesh=mesh, in_specs=in_specs, out_specs=out_specs, check_vma=False)
```

```python
import math

import jax
import jax.numpy as jnp
from jax import lax
from jax.experimental import pallas as pl
from jax.experimental.pallas import tpu as pltpu
from jax.sharding import PartitionSpec as P

HD = 128
PAIR = 2 * HD
MESH = pl.DeviceIdType.MESH
N_Y = 4
N_SEQ = 4
N_SMP = 8
N_X = N_SMP // 2
SUBS = 5
X_CUTS = 4
WINDOW = 2
OUT_CUTS = 4
AT_J1 = 1
AT_I2 = 2
AT_J2 = 3
LAG = 5
KV_ON = 12
KV_END = 14
X_START = (3, 5, 7, 9)
X_STEPS = (11, 15, 19, 23, 16, 20, 24, 27, 28, 30)
PARTNER_AT = (15, 15, 16, 16, 16, 17, 17, 18, 18, 19)
ATTEND_AT = (19, 19, 19, 19, 19, 19, 19, 19)
I1, J1, I2, J2, Y = 0, 1, 2, 3, 4


def reached(i, steps):
    return sum((i >= step).astype(jnp.int32) for step in steps)


def chunk_at(i):
    return jnp.where((i < 3) | (i > 5), i, jnp.where(i == 3, SUBS, i - 1))


def dot(a, b):
    return jnp.dot(a, b, preferred_element_type=jnp.float32)


def dot_t(a, b):
    return lax.dot_general(a, b, (((1,), (1,)), ((), ())), preferred_element_type=jnp.float32)


def kernel(
    px_ref, sx_ref, wq_ref, wk_ref, wv_ref, qg_ref, kg_ref,
    out_ref, dout_ref,
    xb, xp, sxb, w, proj, projp, qsend, tabs, gains, kvx, vaug, kvd, qbuf, obuf, dsend, dec_ref,
    load_sem, x_sem, o_sem, send_sem, recv_sem, kv_send, kv_recv, d_send, d_recv, xs_send, xs_recv, q_send, q_recv,
):
    rows = px_ref.shape[0]
    drows = sx_ref.shape[0] * sx_ref.shape[1]
    heads = wq_ref.shape[1] // HD
    shared = heads // 2
    depth = wq_ref.shape[0] // SUBS
    width = N_SEQ * depth
    chunks = SUBS * (1 + shared // 2)
    count = rows + drows
    half = depth // 2
    quarter = depth // 4
    grp = lax.axis_index("grp")
    seq = lax.axis_index("seq")
    smp = lax.axis_index("smp")
    lo = grp // N_Y
    y = lax.rem(grp, N_Y)
    par = lax.rem(y, 2)
    up = lax.rem(seq + 1, N_SEQ)
    down = lax.rem(seq + N_SEQ - 1, N_SEQ)
    far = lax.rem(seq + 2, N_SEQ)
    mirror = seq + 1 - 2 * lax.rem(seq, 2)
    decodes = (seq == 1) | (seq == 2)
    near = lax.rem(seq + 2 * lo + N_SEQ - 1, N_SEQ)
    other = lax.rem(seq + N_SEQ + 1 - 2 * lo, N_SEQ)
    lo_grp = (1 - lo) * N_Y + y
    inter = (lo_grp, near, smp)
    intra = (lo_grp, seq, smp)
    y_up = lax.rem(y + 1, N_Y)
    y_down = lax.rem(y + N_Y - 1, N_Y)
    y_dev = ((lo * N_Y + y_up, seq, smp), (lo * N_Y + y_down, seq, smp))
    side = lax.rem((y + 1) // 2, 2)
    pair = (lo * N_Y + y + 1 - 2 * par, seq, smp)
    ext = (lo * N_Y + lax.rem(y + 2 * par + N_Y - 1, N_Y), seq, smp)
    core = lax.rem(smp, 2)
    x_up = lax.rem(smp // 2 + 1, N_X) * 2 + core
    x_down = lax.rem(smp // 2 + N_X - 1, N_X) * 2 + core
    x_far = lax.rem(smp // 2 + 2, N_X) * 2 + core
    x_dev = ((grp, seq, x_up), (grp, seq, x_down))
    core_dev = (grp, seq, smp + 1 - 2 * core)
    seq_dev = ((grp, up, smp), (grp, down, smp))

    native = pl.ds(pl.multiple_of(seq * depth, 16), depth)
    for c in range(chunks):
        p, part = c // SUBS, pl.ds(c % SUBS * depth, depth)
        if p == 0:
            for n, ref in enumerate((wk_ref, wv_ref)):
                pltpu.make_async_copy(
                    ref.at[part], w.at[c, native, pl.ds(n * HD, HD)], load_sem.at[0]
                ).start()
        else:
            col = pl.multiple_of((side * shared + 2 * p - 2) * HD, HD)
            pltpu.make_async_copy(
                wq_ref.at[part, pl.ds(col, PAIR)], w.at[c, native], load_sem.at[1]
            ).start()
    x_loads = [
        pltpu.make_async_copy(sx_ref, sxb, x_sem.at[0]),
        pltpu.make_async_copy(qg_ref, gains.at[1], x_sem.at[1]),
        pltpu.make_async_copy(kg_ref, gains.at[0], x_sem.at[1]),
    ]
    for sub in range(SUBS):
        for j in range(N_SEQ):
            x_loads.append(
                pltpu.make_async_copy(
                    px_ref.at[:, pl.ds((j * SUBS + sub) * depth, depth)],
                    xb.at[pl.ds(0, rows), pl.ds(sub * width + j * depth, depth)],
                    x_sem.at[2],
                )
            )
    for load in x_loads:
        load.start()

    barrier = pltpu.get_barrier_semaphore()
    for dev in (inter, intra) + y_dev + seq_dev:
        pl.semaphore_signal(barrier, inc=1, device_id=dev, device_id_type=MESH)
    for d in range(1, N_SMP):
        for s in (seq, mirror):
            pl.semaphore_signal(
                barrier, inc=1, device_id=(grp, s, lax.rem(smp + d, N_SMP)), device_id_type=MESH
            )
    pl.semaphore_wait(barrier, 6 + 2 * (N_SMP - 1))

    def message(c, kind, block, start, size, dev):
        ref = w.at[c, pl.ds(pl.multiple_of(block * depth + start, 16), size)]
        return pltpu.make_async_remote_copy(
            src_ref=ref, dst_ref=ref, send_sem=send_sem.at[kind], recv_sem=recv_sem.at[c, kind],
            device_id=dev, device_id_type=MESH,
        )

    mine = par * half
    theirs = (1 - par) * half

    def send_i1(c):
        for n, (first, last) in enumerate(((0, SUBS), (SUBS, chunks))):
            @pl.when(c == first)
            def _(n=n, first=first, last=last):
                ref = w.at[pl.ds(first, last - first), native]
                pltpu.make_async_copy(ref, ref, load_sem.at[n]).wait()

        message(c, I1, seq, mine, half, inter).start()

    def send_y(c, block, q):
        start = mine + q * quarter

        @pl.when(c < SUBS)
        def _():
            for n in range(2):
                @pl.when(q == n)
                def _():
                    message(c, Y, block, start, quarter, y_dev[n]).start()

        @pl.when(c >= SUBS)
        def _():
            message(c, Y, block, start, quarter, ext).start()

    def arrived(c, kind, block, start, size):
        message(c, kind, block, start, size, inter).wait_recv()

    for c in range(WINDOW):
        send_i1(chunk_at(jnp.int32(c)))

    rblock = count // X_CUTS
    share = SUBS * width // N_SMP

    core_sem = 4 * X_CUTS

    def x_message(n, buf, m, r, dev):
        at = (pl.ds(r * rblock, rblock), pl.ds(pl.multiple_of(m * share, HD), share))
        return pltpu.make_async_remote_copy(
            src_ref=buf.at[at], dst_ref=xp.at[at], send_sem=xs_send, recv_sem=xs_recv.at[n],
            device_id=dev, device_id_type=MESH,
        )

    def x_pair(r):
        return x_message(r, xb, smp, r, pair)

    def x_ring(way, r):
        return x_message((1 + way) * X_CUTS + r, xp, smp, r, x_dev[way])

    def x_fwd(way, r):
        return x_message(3 * X_CUTS + r, xp, (x_down, x_up)[way], r, x_dev[way])

    def x_core(k, r):
        return x_message(core_sem, xp, (smp, x_down, x_up, x_far)[k], r, core_dev)

    def x_step(n):
        stage, r = n // X_CUTS, n % X_CUTS
        if stage == 0:
            x_pair(r).wait_recv()
            x_ring(0, r).start()
            x_ring(1, r).start()
            x_core(0, r).start()
        elif stage == 1:
            for way in range(2):
                x_ring(way, r).wait_recv()
                if r // 2 == way:
                    x_fwd(way, r).start()
                x_core(1 + way, r).start()
        else:
            for way in range(2):
                x_fwd(way, 2 * way + r).wait_recv()
                x_core(3, 2 * way + r).start()

    def x_finish():
        ref = xp.at[:, pl.ds(0, N_X * share)]
        pltpu.make_async_copy(ref, ref, xs_recv.at[core_sem]).wait()

    def x_sent():
        pltpu.make_async_copy(xp, xp, xs_send).wait()

    def start_x():
        for n, ref in enumerate((sxb, gains, xb.at[pl.ds(0, rows)])):
            pltpu.make_async_copy(ref, ref, x_sem.at[n]).wait()
        for sub in range(SUBS):
            for j in range(N_SEQ):
                cols = (j * SUBS + sub) * depth
                at = sub * width + j * depth
                xb[rows:, at : at + depth] = sxb[:, :, cols : cols + depth].reshape(drows, depth)

    def prepare():
        row = lax.broadcasted_iota(jnp.int32, (count, HD), 0)
        lane = lax.broadcasted_iota(jnp.int32, (count, HD), 1)
        index = lax.rem(lane, HD // 2).astype(jnp.float32)
        freq = jnp.exp(index * (-2.0 * math.log(1e6) / HD))
        position = jnp.where(row < rows, seq * rows + row, N_SEQ * rows + lax.rem(row - rows, 4))
        angle = position.astype(jnp.float32) * freq
        cosine = jnp.cos(angle)
        sine = jnp.sin(angle)
        sine = jnp.where(lane < HD // 2, -sine, sine)
        fold = HD ** (-0.5)
        for n, factor in enumerate((1.0, fold)):
            gain = gains[n] * factor
            tabs[n, 0] = cosine * gain
            tabs[n, 1] = sine * pltpu.roll(gain, HD // 2, 1)
        vaug[:, :, HD:] = jnp.ones((N_SEQ, rows, HD), jnp.bfloat16)
        kvd[1, :, HD:] = jnp.ones((drows, HD), jnp.bfloat16)

    def rotated(n, u):
        r = lax.rsqrt(jnp.mean(u * u, -1, keepdims=True) + 1e-6)
        return (r * (u * tabs[n, 0] + pltpu.roll(u, HD // 2, 1) * tabs[n, 1])).astype(jnp.bfloat16)

    def kv_message(n, src, dev):
        return pltpu.make_async_remote_copy(
            src_ref=src, dst_ref=src, send_sem=kv_send, recv_sem=kv_recv.at[n], device_id=dev, device_id_type=MESH
        )

    def kv_own(part, way):
        return kv_message(0, kvx.at[seq, part], seq_dev[way])

    def kv_far(part):
        return kv_message(1, kvx.at[(down, up)[part], part], seq_dev[part])

    def kv_wait(n, blocks):
        ref = kvx.at[pl.ds(0, blocks)]
        pltpu.make_async_copy(ref, ref, (kv_recv.at[0], kv_recv.at[1], kv_send)[n]).wait()

    def out_copy(h):
        return pltpu.make_async_copy(
            obuf.at[h], out_ref.at[:, pl.ds(pl.multiple_of(h * HD, HD), HD)], o_sem
        )

    tile = rows // 2

    def attend_blocks(h, full):
        for r in range(2):
            q = qbuf[h, pl.ds(r * tile, tile)]
            e = jnp.exp(dot_t(q, kvx[full, 0, pl.ds(r * tile, tile)]))
            allowed = lax.broadcasted_iota(jnp.int32, (tile, tile), 1) <= lax.broadcasted_iota(
                jnp.int32, (tile, tile), 0
            )
            e = jnp.where(allowed, e, 0.0).astype(jnp.bfloat16)
            total = dot(e, vaug[full, pl.ds(r * tile, tile)])
            if r > 0:
                e = jnp.exp(dot_t(q, kvx[full, 0, pl.ds(0, tile)])).astype(jnp.bfloat16)
                total += dot(e, vaug[full, pl.ds(0, tile)])
            for j in range(full):
                e = jnp.exp(dot_t(q, kvx[j, 0])).astype(jnp.bfloat16)
                total += dot(e, vaug[j])
            obuf[h, pl.ds(r * tile, tile)] = (total[:, :HD] / total[:, HD:]).astype(jnp.bfloat16)

    def attend_samples(h):
        q = qbuf[h, pl.ds(rows, drows)]
        a = lax.broadcasted_iota(jnp.int32, (drows, drows), 0)
        b = lax.broadcasted_iota(jnp.int32, (drows, drows), 1)
        own = jnp.where((b <= a) & (a // 4 == b // 4), jnp.exp(dot_t(q, kvd[0, :, :HD])), 0.0)
        total = dot(own.astype(jnp.bfloat16), kvd[1])
        for j in range(N_SEQ):
            total += dot(jnp.exp(dot_t(q, kvx[j, 0])).astype(jnp.bfloat16), vaug[j])
        res = total[:, :HD] / total[:, HD:]
        dsend[:, :, :, pl.ds(pl.multiple_of(h * HD, HD), HD)] = res.reshape(dsend.shape[:3] + (HD,))

    def attend(h):
        for full in range(N_SEQ):
            @pl.when(seq == full)
            def _(full=full):
                attend_blocks(h, full)

        out_copy(h).start()

    cols = heads * HD

    def d_message(g, n, to_seq, target):
        first = jnp.where(g < shared // 2, side, 1 - side) * shared + lax.rem(g, shared // 2) * 2
        col = pl.multiple_of(first * HD, HD)
        return pltpu.make_async_remote_copy(
            src_ref=dsend.at[target, :, :, pl.ds(col, PAIR)],
            dst_ref=dec_ref.at[:, :, pl.ds(pl.multiple_of(smp * cols + col, HD), PAIR)],
            send_sem=d_send.at[n], recv_sem=d_recv.at[n],
            device_id=(grp, to_seq, target), device_id_type=MESH,
        )

    def q_message(j):
        return pltpu.make_async_remote_copy(
            src_ref=qsend.at[j], dst_ref=qbuf.at[side * shared + j], send_sem=q_send, recv_sem=q_recv.at[j],
            device_id=pair, device_id_type=MESH,
        )

    def x_cols(sub):
        return pl.ds(pl.multiple_of(sub * width, HD), width)

    def accumulate(ref, x_ref, c):
        sub = lax.rem(c, SUBS)
        part = dot(x_ref[:, x_cols(sub)], w[c])

        @pl.when(sub == 0)
        def _():
            ref[...] = part

        @pl.when(sub > 0)
        def _():
            ref[...] += part

    def partner(n, _):
        accumulate(projp, xp, SUBS + n)

        @pl.when(lax.rem(n, SUBS) == SUBS - 1)
        def _():
            for k in range(2):
                j = n // SUBS * 2 + k
                qsend[j] = rotated(1, projp[:, k * HD : (k + 1) * HD])
                q_message(j).start()

        return 0

    def one(n, _):
        g = n // 2
        received = g >= shared // 2
        j = lax.rem(g, shared // 2) * 2
        first = jnp.where(received, 1 - side, side) * shared + j
        opening = lax.rem(n, 2) == 0

        @pl.when(opening & received)
        def _():
            q_message(j).wait_recv()
            q_message(j + 1).wait_recv()

        @pl.when(opening & (decodes | (g == shared - 1)))
        def _():
            attend_samples(first)
            attend_samples(first + 1)
            for d in range(1, N_SMP):
                d_message(g, 0, seq, lax.rem(smp + d, N_SMP)).start()

        @pl.when(opening & decodes & (g < shared - 1))
        def _():
            for d in range(N_SMP):
                d_message(g, 1, mirror, lax.rem(smp + d, N_SMP)).start()

        attend(first + lax.rem(n, 2))
        return 0

    def x_place(place):
        @pl.when((place >= min(X_STEPS)) & (place <= max(X_STEPS)))
        def _():
            for n, at in enumerate(X_STEPS):
                @pl.when(place == at)
                def _(n=n):
                    x_step(n)

    def step(i, _):
        t = chunk_at(i - LAG)
        new = chunk_at(i)

        @pl.when(i < chunks)
        def _():
            arrived(new, I1, near, mine, half)
            message(new, J1, near, mine, half, intra).start()
            for q in range(2):
                send_y(new, near, q)

        @pl.when(i + WINDOW < chunks)
        def _():
            send_i1(chunk_at(i + WINDOW))

        @pl.when(i == 0)
        def _():
            start_x()

        for n, at in enumerate(X_START):
            @pl.when(i == at)
            def _(n=n):
                x_pair(n).start()

        @pl.when((i >= AT_J1) & (i - AT_J1 < chunks))
        def _():
            c = chunk_at(i - AT_J1)
            arrived(c, J1, other, mine, half)
            message(c, I2, other, mine + (1 - lo) * quarter, quarter, inter).start()
            for q in range(2):
                send_y(c, other, q)

        x_place(2 * i)

        @pl.when((i >= AT_I2) & (i - AT_I2 < chunks))
        def _():
            c = chunk_at(i - AT_I2)
            arrived(c, I2, far, mine + lo * quarter, quarter)
            message(c, J2, far, mine + lo * quarter, quarter, intra).start()
            send_y(c, far, lo)

        @pl.when((i >= AT_J2) & (i - AT_J2 < chunks))
        def _():
            c = chunk_at(i - AT_J2)
            arrived(c, J2, far, mine + (1 - lo) * quarter, quarter)
            send_y(c, far, 1 - lo)

        @pl.when(i == 1)
        def _():
            prepare()

        @pl.when(i == KV_ON)
        def _():
            kv_wait(0, 2)
            for part in range(2):
                kv_far(part).start()

        active = i >= LAG

        @pl.when(active)
        def _():
            message(t, Y, 0, 0, 3 * half, inter).wait_recv()

        x_place(2 * i + 1)

        @pl.when(i == PARTNER_AT[0])
        def _():
            x_finish()

        lax.fori_loop(reached(i - 1, PARTNER_AT), reached(i, PARTNER_AT), partner, 0)

        @pl.when(active)
        def _():
            accumulate(proj.at[jnp.minimum(t // SUBS, 1)], xb, t)

            @pl.when(t == SUBS - 1)
            def _():
                k = rotated(0, proj[0, :, :HD])
                v = proj[0, :, HD:].astype(jnp.bfloat16)
                kvx[seq, 0] = k[:rows]
                kvx[seq, 1] = v[:rows]
                kvd[0, :, :HD] = k[rows:]
                kvd[1, :, :HD] = v[rows:]
                for part in range(2):
                    for way in range(2):
                        kv_own(part, way).start()

            @pl.when((t >= SUBS) & (lax.rem(t, SUBS) == SUBS - 1))
            def _():
                for k in range(2):
                    qbuf[side * shared + (t // SUBS - 1) * 2 + k] = rotated(1, proj[1, :, k * HD : (k + 1) * HD])

        @pl.when(i == KV_END)
        def _():
            kv_wait(1, 1)
            vaug[:, :, :HD] = kvx[:, 1]

        lax.fori_loop(reached(i - 1, ATTEND_AT), reached(i, ATTEND_AT), one, 0)
        return 0

    lax.fori_loop(0, chunks + LAG, step, 0)

    @pl.when(decodes)
    def _():
        dec_ref[:, :, pl.ds(pl.multiple_of(smp * cols, HD), cols)] = dsend[smp]

    @pl.when(jnp.logical_not(decodes))
    def _():
        col = pl.multiple_of((1 - side) * shared * HD + (shared - 2) * HD, HD)
        dec_ref[:, :, pl.ds(pl.multiple_of(smp * cols + col, HD), PAIR)] = dsend[smp, :, :, pl.ds(col, PAIR)]

    for kind, size in ((I1, half), (J1, half), (I2, quarter), (J2, quarter), (Y, 3 * half)):
        ref = w.at[:, pl.ds(0, size)]
        pltpu.make_async_remote_copy(
            src_ref=ref, dst_ref=ref, send_sem=send_sem.at[kind], recv_sem=recv_sem.at[0, kind],
            device_id=inter, device_id_type=MESH,
        ).wait_send()
    x_sent()
    pltpu.make_async_copy(qsend, qsend, q_send).wait()
    kv_wait(2, 3)
    pltpu.make_async_copy(obuf, obuf, o_sem).wait()

    early = dsend.at[:, :, :, pl.ds(0, cols - PAIR)]

    @pl.when(decodes)
    def _():
        part = dsend.at[pl.ds(0, N_SMP - 1)]
        pltpu.make_async_copy(early, early, d_send.at[1]).wait()
        pltpu.make_async_copy(part, part, d_send.at[0]).wait()
        pltpu.make_async_copy(part, part, d_recv.at[0]).wait()

    @pl.when(jnp.logical_not(decodes))
    def _():
        part = dsend.at[pl.ds(0, N_SMP - 1), :, :, pl.ds(0, PAIR)]
        pltpu.make_async_copy(part, part, d_send.at[0]).wait()
        pltpu.make_async_copy(early, early, d_recv.at[1]).wait()
        pltpu.make_async_copy(part, part, d_recv.at[0]).wait()

    dout_ref[...] = dec_ref[...].astype(jnp.bfloat16)


def deliver(p_ref, d_ref, out_ref, dec_ref, p_buf, d_buf, sem):
    size = p_ref.shape[0] // OUT_CUTS
    ways = [(d_ref, d_buf, dec_ref)]
    for n in range(OUT_CUTS):
        ways.append(tuple(ref.at[pl.ds(n * size, size)] for ref in (p_ref, p_buf, out_ref)))
    for n, (src, buf, _) in enumerate(ways):
        pltpu.make_async_copy(src, buf, sem.at[0, n]).start()
    for n, (src, buf, dst) in enumerate(ways):
        pltpu.make_async_copy(src, buf, sem.at[0, n]).wait()
        pltpu.make_async_copy(buf, dst, sem.at[1, n]).start()
    for n, (_, buf, dst) in enumerate(ways):
        pltpu.make_async_copy(buf, dst, sem.at[1, n]).wait()


def local(prompt_x, sampled_x, w_query, w_key, w_value, q_gain, k_gain):
    rows, width = prompt_x.shape
    samples, steps, _ = sampled_x.shape
    drows = samples * steps
    q_cols = w_query.shape[1]
    heads = q_cols // HD
    shared = heads // 2
    chunks = SUBS * (1 + shared // 2)
    count = rows + drows
    own = samples // N_SMP
    hbm = pl.BlockSpec(memory_space=pltpu.HBM)
    vmem = pl.BlockSpec(memory_space=pltpu.VMEM)
    dma = pltpu.SemaphoreType.DMA
    prefill, dec = pl.pallas_call(
        kernel,
        out_shape=(
            jax.ShapeDtypeStruct((rows, q_cols), jnp.bfloat16),
            jax.ShapeDtypeStruct((own, steps, N_SMP * q_cols), jnp.bfloat16),
        ),
        in_specs=[hbm] * 7,
        out_specs=(pl.BlockSpec(memory_space=pl.ANY), vmem),
        scratch_shapes=[
            pltpu.VMEM((count, width), jnp.bfloat16),
            pltpu.VMEM((count, width), jnp.bfloat16),
            pltpu.VMEM((samples, steps, width), jnp.bfloat16),
            pltpu.VMEM((chunks, width // SUBS, PAIR), jnp.bfloat16),
            pltpu.VMEM((2, count, PAIR), jnp.float32),
            pltpu.VMEM((count, PAIR), jnp.float32),
            pltpu.VMEM((shared, count, HD), jnp.bfloat16),
            pltpu.VMEM((2, 2, count, HD), jnp.float32),
            pltpu.VMEM((2, 1, HD), jnp.float32),
            pltpu.VMEM((N_SEQ, 2, rows, HD), jnp.bfloat16),
            pltpu.VMEM((N_SEQ, rows, PAIR), jnp.bfloat16),
            pltpu.VMEM((2, drows, PAIR), jnp.bfloat16),
            pltpu.VMEM((heads, count, HD), jnp.bfloat16),
            pltpu.VMEM((heads, rows, HD), jnp.bfloat16),
            pltpu.VMEM((N_SMP, own, steps, q_cols), jnp.float32),
            pltpu.VMEM((own, steps, N_SMP * q_cols), jnp.float32),
            dma((2,)),
            dma((3,)),
            dma,
            dma((5,)),
            dma((chunks, 5)),
            dma,
            dma((2,)),
            dma((2,)),
            dma((2,)),
            dma,
            dma((4 * X_CUTS + 1,)),
            dma,
            dma((shared,)),
        ],
        compiler_params=pltpu.CompilerParams(
            collective_id=0, has_side_effects=True, vmem_limit_bytes=58 * 2**20
        ),
    )(prompt_x, sampled_x, w_query, w_key, w_value, q_gain.reshape(1, HD), k_gain.reshape(1, HD))
    return pl.pallas_call(
        deliver,
        out_shape=(
            jax.ShapeDtypeStruct((rows, q_cols), jnp.bfloat16),
            jax.ShapeDtypeStruct((own, steps, N_SMP * q_cols), jnp.bfloat16),
        ),
        in_specs=[hbm, hbm],
        out_specs=(hbm, hbm),
        scratch_shapes=[
            pltpu.VMEM((rows, q_cols), jnp.bfloat16),
            pltpu.VMEM((own, steps, N_SMP * q_cols), jnp.bfloat16),
            dma((2, 1 + OUT_CUTS)),
        ],
        compiler_params=pltpu.CompilerParams(vmem_limit_bytes=58 * 2**20),
    )(prefill, dec)


def solution(mesh):
    in_specs = (
        P(("grp", "seq"), None),
        P("grp", None, None),
        P("seq", "smp"),
        P("seq", "smp"),
        P("seq", "smp"),
        P(),
        P(),
    )
    out_specs = (P(("grp", "seq"), "smp"), P(("grp", "smp"), None, None))
    return jax.shard_map(local, mesh=mesh, in_specs=in_specs, out_specs=out_specs, check_vma=False)
```

```python
import math

import jax
import jax.numpy as jnp
from jax import lax
from jax.experimental import pallas as pl
from jax.experimental.pallas import tpu as pltpu
from jax.sharding import PartitionSpec as P

HD = 128
PAIR = 2 * HD
MESH = pl.DeviceIdType.MESH
N_Y = 4
N_SEQ = 4
N_SMP = 8
N_X = N_SMP // 2
SUBS = 5
X_CUTS = 4
WINDOW = 2
OUT_CUTS = 4
AT_J1 = 1
AT_I2 = 2
AT_J2 = 3
LAG = 5
KV_AT = (12, 13)
KV_ON = 16
KV_END = 18
X_START = (3, 5, 7, 9)
X_STEPS = (11, 15, 19, 23, 16, 20, 24, 27, 28, 30)
PARTNER_AT = (15, 15, 16, 16, 16, 17, 17, 18, 18, 19)
ATTEND_AT = (19, 19, 19, 19, 19, 19, 19, 19)
I1, J1, I2, J2, Y = 0, 1, 2, 3, 4


def reached(i, steps):
    return sum((i >= step).astype(jnp.int32) for step in steps)


def chunk_at(i):
    return jnp.where((i < 3) | (i > 5), i, jnp.where(i == 3, SUBS, i - 1))


def dot(a, b):
    return jnp.dot(a, b, preferred_element_type=jnp.float32)


def dot_t(a, b):
    return lax.dot_general(a, b, (((1,), (1,)), ((), ())), preferred_element_type=jnp.float32)


def kernel(
    px_ref, sx_ref, wq_ref, wk_ref, wv_ref, qg_ref, kg_ref,
    out_ref, dout_ref,
    xb, xp, sxb, w, proj, projp, qsend, tabs, gains, kvx, vaug, kvd, qbuf, obuf, dsend, dec_ref,
    load_sem, x_sem, o_sem, send_sem, recv_sem, kv_send, kv_recv, d_send, d_recv, xs_send, xs_recv, q_send, q_recv,
):
    rows = px_ref.shape[0]
    drows = sx_ref.shape[0] * sx_ref.shape[1]
    heads = wq_ref.shape[1] // HD
    shared = heads // 2
    depth = wq_ref.shape[0] // SUBS
    width = N_SEQ * depth
    chunks = SUBS * (1 + shared // 2)
    count = rows + drows
    half = depth // 2
    quarter = depth // 4
    grp = lax.axis_index("grp")
    seq = lax.axis_index("seq")
    smp = lax.axis_index("smp")
    lo = grp // N_Y
    y = lax.rem(grp, N_Y)
    par = lax.rem(y, 2)
    up = lax.rem(seq + 1, N_SEQ)
    down = lax.rem(seq + N_SEQ - 1, N_SEQ)
    far = lax.rem(seq + 2, N_SEQ)
    mirror = seq + 1 - 2 * lax.rem(seq, 2)
    decodes = (seq == 1) | (seq == 2)
    near = lax.rem(seq + 2 * lo + N_SEQ - 1, N_SEQ)
    other = lax.rem(seq + N_SEQ + 1 - 2 * lo, N_SEQ)
    lo_grp = (1 - lo) * N_Y + y
    inter = (lo_grp, near, smp)
    intra = (lo_grp, seq, smp)
    y_up = lax.rem(y + 1, N_Y)
    y_down = lax.rem(y + N_Y - 1, N_Y)
    y_dev = ((lo * N_Y + y_up, seq, smp), (lo * N_Y + y_down, seq, smp))
    side = lax.rem((y + 1) // 2, 2)
    pair = (lo * N_Y + y + 1 - 2 * par, seq, smp)
    ext = (lo * N_Y + lax.rem(y + 2 * par + N_Y - 1, N_Y), seq, smp)
    core = lax.rem(smp, 2)
    x_up = lax.rem(smp // 2 + 1, N_X) * 2 + core
    x_down = lax.rem(smp // 2 + N_X - 1, N_X) * 2 + core
    x_far = lax.rem(smp // 2 + 2, N_X) * 2 + core
    x_dev = ((grp, seq, x_up), (grp, seq, x_down))
    core_dev = (grp, seq, smp + 1 - 2 * core)
    seq_dev = ((grp, up, smp), (grp, down, smp))

    native = pl.ds(pl.multiple_of(seq * depth, 16), depth)
    for c in range(chunks):
        p, part = c // SUBS, pl.ds(c % SUBS * depth, depth)
        if p == 0:
            for n, ref in enumerate((wk_ref, wv_ref)):
                pltpu.make_async_copy(
                    ref.at[part], w.at[c, native, pl.ds(n * HD, HD)], load_sem.at[0]
                ).start()
        else:
            col = pl.multiple_of((side * shared + 2 * p - 2) * HD, HD)
            pltpu.make_async_copy(
                wq_ref.at[part, pl.ds(col, PAIR)], w.at[c, native], load_sem.at[1]
            ).start()
    x_loads = [
        pltpu.make_async_copy(sx_ref, sxb, x_sem.at[0]),
        pltpu.make_async_copy(qg_ref, gains.at[1], x_sem.at[1]),
        pltpu.make_async_copy(kg_ref, gains.at[0], x_sem.at[1]),
    ]
    for sub in range(SUBS):
        for j in range(N_SEQ):
            x_loads.append(
                pltpu.make_async_copy(
                    px_ref.at[:, pl.ds((j * SUBS + sub) * depth, depth)],
                    xb.at[pl.ds(0, rows), pl.ds(sub * width + j * depth, depth)],
                    x_sem.at[2],
                )
            )
    for load in x_loads:
        load.start()

    barrier = pltpu.get_barrier_semaphore()
    for dev in (inter, intra) + y_dev + seq_dev:
        pl.semaphore_signal(barrier, inc=1, device_id=dev, device_id_type=MESH)
    for d in range(1, N_SMP):
        for s in (seq, mirror):
            pl.semaphore_signal(
                barrier, inc=1, device_id=(grp, s, lax.rem(smp + d, N_SMP)), device_id_type=MESH
            )
    pl.semaphore_wait(barrier, 6 + 2 * (N_SMP - 1))

    def message(c, kind, block, start, size, dev):
        ref = w.at[c, pl.ds(pl.multiple_of(block * depth + start, 16), size)]
        return pltpu.make_async_remote_copy(
            src_ref=ref, dst_ref=ref, send_sem=send_sem.at[kind], recv_sem=recv_sem.at[c, kind],
            device_id=dev, device_id_type=MESH,
        )

    mine = par * half
    theirs = (1 - par) * half

    def send_i1(c):
        for n, (first, last) in enumerate(((0, SUBS), (SUBS, chunks))):
            @pl.when(c == first)
            def _(n=n, first=first, last=last):
                ref = w.at[pl.ds(first, last - first), native]
                pltpu.make_async_copy(ref, ref, load_sem.at[n]).wait()

        message(c, I1, seq, mine, half, inter).start()

    def send_y(c, block, q):
        start = mine + q * quarter

        @pl.when(c < SUBS)
        def _():
            for n in range(2):
                @pl.when(q == n)
                def _():
                    message(c, Y, block, start, quarter, y_dev[n]).start()

        @pl.when(c >= SUBS)
        def _():
            message(c, Y, block, start, quarter, ext).start()

    def arrived(c, kind, block, start, size):
        message(c, kind, block, start, size, inter).wait_recv()

    for c in range(WINDOW):
        send_i1(chunk_at(jnp.int32(c)))

    rblock = count // X_CUTS
    share = SUBS * width // N_SMP

    core_sem = 4 * X_CUTS

    def x_message(n, buf, m, r, dev):
        at = (pl.ds(r * rblock, rblock), pl.ds(pl.multiple_of(m * share, HD), share))
        return pltpu.make_async_remote_copy(
            src_ref=buf.at[at], dst_ref=xp.at[at], send_sem=xs_send, recv_sem=xs_recv.at[n],
            device_id=dev, device_id_type=MESH,
        )

    def x_pair(r):
        return x_message(r, xb, smp, r, pair)

    def x_ring(way, r):
        return x_message((1 + way) * X_CUTS + r, xp, smp, r, x_dev[way])

    def x_fwd(way, r):
        return x_message(3 * X_CUTS + r, xp, (x_down, x_up)[way], r, x_dev[way])

    def x_core(k, r):
        return x_message(core_sem, xp, (smp, x_down, x_up, x_far)[k], r, core_dev)

    def x_step(n):
        stage, r = n // X_CUTS, n % X_CUTS
        if stage == 0:
            x_pair(r).wait_recv()
            x_ring(0, r).start()
            x_ring(1, r).start()
            x_core(0, r).start()
        elif stage == 1:
            for way in range(2):
                x_ring(way, r).wait_recv()
                if r // 2 == way:
                    x_fwd(way, r).start()
                x_core(1 + way, r).start()
        else:
            for way in range(2):
                x_fwd(way, 2 * way + r).wait_recv()
                x_core(3, 2 * way + r).start()

    def x_finish():
        ref = xp.at[:, pl.ds(0, N_X * share)]
        pltpu.make_async_copy(ref, ref, xs_recv.at[core_sem]).wait()

    def x_sent():
        pltpu.make_async_copy(xp, xp, xs_send).wait()

    def start_x():
        for n, ref in enumerate((sxb, gains, xb.at[pl.ds(0, rows)])):
            pltpu.make_async_copy(ref, ref, x_sem.at[n]).wait()
        for sub in range(SUBS):
            for j in range(N_SEQ):
                cols = (j * SUBS + sub) * depth
                at = sub * width + j * depth
                xb[rows:, at : at + depth] = sxb[:, :, cols : cols + depth].reshape(drows, depth)

    def prepare():
        row = lax.broadcasted_iota(jnp.int32, (count, HD), 0)
        lane = lax.broadcasted_iota(jnp.int32, (count, HD), 1)
        index = lax.rem(lane, HD // 2).astype(jnp.float32)
        freq = jnp.exp(index * (-2.0 * math.log(1e6) / HD))
        position = jnp.where(row < rows, seq * rows + row, N_SEQ * rows + lax.rem(row - rows, 4))
        angle = position.astype(jnp.float32) * freq
        cosine = jnp.cos(angle)
        sine = jnp.sin(angle)
        sine = jnp.where(lane < HD // 2, -sine, sine)
        fold = HD ** (-0.5)
        for n, factor in enumerate((1.0, fold)):
            gain = gains[n] * factor
            tabs[n, 0] = cosine * gain
            tabs[n, 1] = sine * pltpu.roll(gain, HD // 2, 1)
        vaug[:, :, HD:] = jnp.ones((N_SEQ, rows, HD), jnp.bfloat16)
        kvd[1, :, HD:] = jnp.ones((drows, HD), jnp.bfloat16)

    def rotated(n, u):
        r = lax.rsqrt(jnp.mean(u * u, -1, keepdims=True) + 1e-6)
        return (r * (u * tabs[n, 0] + pltpu.roll(u, HD // 2, 1) * tabs[n, 1])).astype(jnp.bfloat16)

    def kv_message(n, src, dev):
        return pltpu.make_async_remote_copy(
            src_ref=src, dst_ref=src, send_sem=kv_send, recv_sem=kv_recv.at[n], device_id=dev, device_id_type=MESH
        )

    def kv_own(part, way):
        return kv_message(0, kvx.at[seq, part], seq_dev[way])

    def kv_far(part):
        return kv_message(1, kvx.at[(down, up)[part], part], seq_dev[part])

    def kv_wait(n, blocks):
        ref = kvx.at[pl.ds(0, blocks)]
        pltpu.make_async_copy(ref, ref, (kv_recv.at[0], kv_recv.at[1], kv_send)[n]).wait()

    def out_copy(h):
        return pltpu.make_async_copy(
            obuf.at[h], out_ref.at[:, pl.ds(pl.multiple_of(h * HD, HD), HD)], o_sem
        )

    tile = rows // 2

    def attend_blocks(h, full):
        for r in range(2):
            q = qbuf[h, pl.ds(r * tile, tile)]
            e = jnp.exp(dot_t(q, kvx[full, 0, pl.ds(r * tile, tile)]))
            allowed = lax.broadcasted_iota(jnp.int32, (tile, tile), 1) <= lax.broadcasted_iota(
                jnp.int32, (tile, tile), 0
            )
            e = jnp.where(allowed, e, 0.0).astype(jnp.bfloat16)
            total = dot(e, vaug[full, pl.ds(r * tile, tile)])
            if r > 0:
                e = jnp.exp(dot_t(q, kvx[full, 0, pl.ds(0, tile)])).astype(jnp.bfloat16)
                total += dot(e, vaug[full, pl.ds(0, tile)])
            for j in range(full):
                e = jnp.exp(dot_t(q, kvx[j, 0])).astype(jnp.bfloat16)
                total += dot(e, vaug[j])
            obuf[h, pl.ds(r * tile, tile)] = (total[:, :HD] / total[:, HD:]).astype(jnp.bfloat16)

    def attend_samples(h):
        q = qbuf[h, pl.ds(rows, drows)]
        a = lax.broadcasted_iota(jnp.int32, (drows, drows), 0)
        b = lax.broadcasted_iota(jnp.int32, (drows, drows), 1)
        own = jnp.where((b <= a) & (a // 4 == b // 4), jnp.exp(dot_t(q, kvd[0, :, :HD])), 0.0)
        total = dot(own.astype(jnp.bfloat16), kvd[1])
        for j in range(N_SEQ):
            total += dot(jnp.exp(dot_t(q, kvx[j, 0])).astype(jnp.bfloat16), vaug[j])
        res = total[:, :HD] / total[:, HD:]
        dsend[:, :, :, pl.ds(pl.multiple_of(h * HD, HD), HD)] = res.reshape(dsend.shape[:3] + (HD,))

    def attend(h):
        for full in range(N_SEQ):
            @pl.when(seq == full)
            def _(full=full):
                attend_blocks(h, full)

        out_copy(h).start()

    cols = heads * HD

    def d_message(g, n, to_seq, target):
        first = jnp.where(g < shared // 2, side, 1 - side) * shared + lax.rem(g, shared // 2) * 2
        col = pl.multiple_of(first * HD, HD)
        return pltpu.make_async_remote_copy(
            src_ref=dsend.at[target, :, :, pl.ds(col, PAIR)],
            dst_ref=dec_ref.at[:, :, pl.ds(pl.multiple_of(smp * cols + col, HD), PAIR)],
            send_sem=d_send.at[n], recv_sem=d_recv.at[n],
            device_id=(grp, to_seq, target), device_id_type=MESH,
        )

    def q_message(j):
        return pltpu.make_async_remote_copy(
            src_ref=qsend.at[j], dst_ref=qbuf.at[side * shared + j], send_sem=q_send, recv_sem=q_recv.at[j],
            device_id=pair, device_id_type=MESH,
        )

    def x_cols(sub):
        return pl.ds(pl.multiple_of(sub * width, HD), width)

    def accumulate(ref, x_ref, c):
        sub = lax.rem(c, SUBS)
        part = dot(x_ref[:, x_cols(sub)], w[c])

        @pl.when(sub == 0)
        def _():
            ref[...] = part

        @pl.when(sub > 0)
        def _():
            ref[...] += part

    def partner(n, _):
        accumulate(projp, xp, SUBS + n)

        @pl.when(lax.rem(n, SUBS) == SUBS - 1)
        def _():
            for k in range(2):
                j = n // SUBS * 2 + k
                qsend[j] = rotated(1, projp[:, k * HD : (k + 1) * HD])
                q_message(j).start()

        return 0

    def one(n, _):
        g = n // 2
        received = g >= shared // 2
        j = lax.rem(g, shared // 2) * 2
        first = jnp.where(received, 1 - side, side) * shared + j
        opening = lax.rem(n, 2) == 0

        @pl.when(opening & received)
        def _():
            q_message(j).wait_recv()
            q_message(j + 1).wait_recv()

        @pl.when(opening & (decodes | (g == shared - 1)))
        def _():
            attend_samples(first)
            attend_samples(first + 1)
            for d in range(1, N_SMP):
                d_message(g, 0, seq, lax.rem(smp + d, N_SMP)).start()

        @pl.when(opening & decodes & (g < shared - 1))
        def _():
            for d in range(N_SMP):
                d_message(g, 1, mirror, lax.rem(smp + d, N_SMP)).start()

        attend(first + lax.rem(n, 2))
        return 0

    def x_place(place):
        @pl.when((place >= min(X_STEPS)) & (place <= max(X_STEPS)))
        def _():
            for n, at in enumerate(X_STEPS):
                @pl.when(place == at)
                def _(n=n):
                    x_step(n)

    def step(i, _):
        t = chunk_at(i - LAG)
        new = chunk_at(i)

        @pl.when(i < chunks)
        def _():
            arrived(new, I1, near, mine, half)
            message(new, J1, near, mine, half, intra).start()
            for q in range(2):
                send_y(new, near, q)

        @pl.when(i + WINDOW < chunks)
        def _():
            send_i1(chunk_at(i + WINDOW))

        @pl.when(i == 0)
        def _():
            start_x()

        for n, at in enumerate(X_START):
            @pl.when(i == at)
            def _(n=n):
                x_pair(n).start()

        @pl.when((i >= AT_J1) & (i - AT_J1 < chunks))
        def _():
            c = chunk_at(i - AT_J1)
            arrived(c, J1, other, mine, half)
            message(c, I2, other, mine + (1 - lo) * quarter, quarter, inter).start()
            for q in range(2):
                send_y(c, other, q)

        x_place(2 * i)

        @pl.when((i >= AT_I2) & (i - AT_I2 < chunks))
        def _():
            c = chunk_at(i - AT_I2)
            arrived(c, I2, far, mine + lo * quarter, quarter)
            message(c, J2, far, mine + lo * quarter, quarter, intra).start()
            send_y(c, far, lo)

        @pl.when((i >= AT_J2) & (i - AT_J2 < chunks))
        def _():
            c = chunk_at(i - AT_J2)
            arrived(c, J2, far, mine + (1 - lo) * quarter, quarter)
            send_y(c, far, 1 - lo)

        @pl.when(i == 1)
        def _():
            prepare()

        @pl.when(i == KV_ON)
        def _():
            kv_wait(0, 2)
            for part in range(2):
                kv_far(part).start()

        active = i >= LAG

        @pl.when(active)
        def _():
            message(t, Y, 0, 0, 3 * half, inter).wait_recv()

        x_place(2 * i + 1)

        @pl.when(i == PARTNER_AT[0])
        def _():
            x_finish()

        lax.fori_loop(reached(i - 1, PARTNER_AT), reached(i, PARTNER_AT), partner, 0)

        @pl.when(active)
        def _():
            accumulate(proj.at[jnp.minimum(t // SUBS, 1)], xb, t)

            @pl.when(t == SUBS - 1)
            def _():
                k = rotated(0, proj[0, :, :HD])
                v = proj[0, :, HD:].astype(jnp.bfloat16)
                kvx[seq, 0] = k[:rows]
                kvx[seq, 1] = v[:rows]
                kvd[0, :, :HD] = k[rows:]
                kvd[1, :, :HD] = v[rows:]

            @pl.when((t >= SUBS) & (lax.rem(t, SUBS) == SUBS - 1))
            def _():
                for k in range(2):
                    qbuf[side * shared + (t // SUBS - 1) * 2 + k] = rotated(1, proj[1, :, k * HD : (k + 1) * HD])

        for part, at in enumerate(KV_AT):
            @pl.when(i == at)
            def _(part=part):
                for way in range(2):
                    kv_own(part, way).start()

        @pl.when(i == KV_END)
        def _():
            kv_wait(1, 1)
            vaug[:, :, :HD] = kvx[:, 1]

        lax.fori_loop(reached(i - 1, ATTEND_AT), reached(i, ATTEND_AT), one, 0)
        return 0

    lax.fori_loop(0, chunks + LAG, step, 0)

    @pl.when(decodes)
    def _():
        dec_ref[:, :, pl.ds(pl.multiple_of(smp * cols, HD), cols)] = dsend[smp]

    @pl.when(jnp.logical_not(decodes))
    def _():
        col = pl.multiple_of((1 - side) * shared * HD + (shared - 2) * HD, HD)
        dec_ref[:, :, pl.ds(pl.multiple_of(smp * cols + col, HD), PAIR)] = dsend[smp, :, :, pl.ds(col, PAIR)]

    for kind, size in ((I1, half), (J1, half), (I2, quarter), (J2, quarter), (Y, 3 * half)):
        ref = w.at[:, pl.ds(0, size)]
        pltpu.make_async_remote_copy(
            src_ref=ref, dst_ref=ref, send_sem=send_sem.at[kind], recv_sem=recv_sem.at[0, kind],
            device_id=inter, device_id_type=MESH,
        ).wait_send()
    x_sent()
    pltpu.make_async_copy(qsend, qsend, q_send).wait()
    kv_wait(2, 3)
    pltpu.make_async_copy(obuf, obuf, o_sem).wait()

    early = dsend.at[:, :, :, pl.ds(0, cols - PAIR)]

    @pl.when(decodes)
    def _():
        part = dsend.at[pl.ds(0, N_SMP - 1)]
        pltpu.make_async_copy(early, early, d_send.at[1]).wait()
        pltpu.make_async_copy(part, part, d_send.at[0]).wait()
        pltpu.make_async_copy(part, part, d_recv.at[0]).wait()

    @pl.when(jnp.logical_not(decodes))
    def _():
        part = dsend.at[pl.ds(0, N_SMP - 1), :, :, pl.ds(0, PAIR)]
        pltpu.make_async_copy(part, part, d_send.at[0]).wait()
        pltpu.make_async_copy(early, early, d_recv.at[1]).wait()
        pltpu.make_async_copy(part, part, d_recv.at[0]).wait()

    dout_ref[...] = dec_ref[...].astype(jnp.bfloat16)


def deliver(p_ref, d_ref, out_ref, dec_ref, p_buf, d_buf, sem):
    size = p_ref.shape[0] // OUT_CUTS
    ways = [(d_ref, d_buf, dec_ref)]
    for n in range(OUT_CUTS):
        ways.append(tuple(ref.at[pl.ds(n * size, size)] for ref in (p_ref, p_buf, out_ref)))
    for n, (src, buf, _) in enumerate(ways):
        pltpu.make_async_copy(src, buf, sem.at[0, n]).start()
    for n, (src, buf, dst) in enumerate(ways):
        pltpu.make_async_copy(src, buf, sem.at[0, n]).wait()
        pltpu.make_async_copy(buf, dst, sem.at[1, n]).start()
    for n, (_, buf, dst) in enumerate(ways):
        pltpu.make_async_copy(buf, dst, sem.at[1, n]).wait()


def local(prompt_x, sampled_x, w_query, w_key, w_value, q_gain, k_gain):
    rows, width = prompt_x.shape
    samples, steps, _ = sampled_x.shape
    drows = samples * steps
    q_cols = w_query.shape[1]
    heads = q_cols // HD
    shared = heads // 2
    chunks = SUBS * (1 + shared // 2)
    count = rows + drows
    own = samples // N_SMP
    hbm = pl.BlockSpec(memory_space=pltpu.HBM)
    vmem = pl.BlockSpec(memory_space=pltpu.VMEM)
    dma = pltpu.SemaphoreType.DMA
    prefill, dec = pl.pallas_call(
        kernel,
        out_shape=(
            jax.ShapeDtypeStruct((rows, q_cols), jnp.bfloat16),
            jax.ShapeDtypeStruct((own, steps, N_SMP * q_cols), jnp.bfloat16),
        ),
        in_specs=[hbm] * 7,
        out_specs=(pl.BlockSpec(memory_space=pl.ANY), vmem),
        scratch_shapes=[
            pltpu.VMEM((count, width), jnp.bfloat16),
            pltpu.VMEM((count, width), jnp.bfloat16),
            pltpu.VMEM((samples, steps, width), jnp.bfloat16),
            pltpu.VMEM((chunks, width // SUBS, PAIR), jnp.bfloat16),
            pltpu.VMEM((2, count, PAIR), jnp.float32),
            pltpu.VMEM((count, PAIR), jnp.float32),
            pltpu.VMEM((shared, count, HD), jnp.bfloat16),
            pltpu.VMEM((2, 2, count, HD), jnp.float32),
            pltpu.VMEM((2, 1, HD), jnp.float32),
            pltpu.VMEM((N_SEQ, 2, rows, HD), jnp.bfloat16),
            pltpu.VMEM((N_SEQ, rows, PAIR), jnp.bfloat16),
            pltpu.VMEM((2, drows, PAIR), jnp.bfloat16),
            pltpu.VMEM((heads, count, HD), jnp.bfloat16),
            pltpu.VMEM((heads, rows, HD), jnp.bfloat16),
            pltpu.VMEM((N_SMP, own, steps, q_cols), jnp.float32),
            pltpu.VMEM((own, steps, N_SMP * q_cols), jnp.float32),
            dma((2,)),
            dma((3,)),
            dma,
            dma((5,)),
            dma((chunks, 5)),
            dma,
            dma((2,)),
            dma((2,)),
            dma((2,)),
            dma,
            dma((4 * X_CUTS + 1,)),
            dma,
            dma((shared,)),
        ],
        compiler_params=pltpu.CompilerParams(
            collective_id=0, has_side_effects=True, vmem_limit_bytes=58 * 2**20
        ),
    )(prompt_x, sampled_x, w_query, w_key, w_value, q_gain.reshape(1, HD), k_gain.reshape(1, HD))
    return pl.pallas_call(
        deliver,
        out_shape=(
            jax.ShapeDtypeStruct((rows, q_cols), jnp.bfloat16),
            jax.ShapeDtypeStruct((own, steps, N_SMP * q_cols), jnp.bfloat16),
        ),
        in_specs=[hbm, hbm],
        out_specs=(hbm, hbm),
        scratch_shapes=[
            pltpu.VMEM((rows, q_cols), jnp.bfloat16),
            pltpu.VMEM((own, steps, N_SMP * q_cols), jnp.bfloat16),
            dma((2, 1 + OUT_CUTS)),
        ],
        compiler_params=pltpu.CompilerParams(vmem_limit_bytes=58 * 2**20),
    )(prefill, dec)


def solution(mesh):
    in_specs = (
        P(("grp", "seq"), None),
        P("grp", None, None),
        P("seq", "smp"),
        P("seq", "smp"),
        P("seq", "smp"),
        P(),
        P(),
    )
    out_specs = (P(("grp", "seq"), "smp"), P(("grp", "smp"), None, None))
    return jax.shard_map(local, mesh=mesh, in_specs=in_specs, out_specs=out_specs, check_vma=False)
```
